512 devices in a mesh: side: 4 (over z_lo), rep: 8 (over x, core), tp: 16 (over z_hi, y).
Axes of the slice: x: 4, y: 8, z: 8 (z_hi: 2, z_lo: 4; z = z_hi * 4 + z_lo), core: 2. Of those that a mesh axis runs over, the one named last changes fastest.
Arguments:
- learn_inputs: bfloat16 [4, 8192, 8192], P('side', 'rep', 'tp'), may hold values from -6 to 6
- learn_grads: bfloat16 [4, 8192, 2048], P('side', ('rep', 'tp')), may hold values from -0.5 to 0.5
- kv_master: float32 [8192, 2048], P('tp', 'rep'), may hold values from -0.0625 to 0.0625
- first_moment: bfloat16 [8192, 2048], P('tp', 'rep'), may hold values from -12 to 12
- second_moment: bfloat16 [8192, 2048], P('tp', 'rep'), may hold values from 0.0099487305 to 0.29882812
- decode_inputs: bfloat16 [512, 8192], P(('side', 'rep'), 'tp'), may hold values from -6 to 6
- queries: bfloat16 [512, 8192], P(('side', 'rep', 'tp')), may hold values from -6 to 6
- key_cache_slots: bfloat16 [512, 128, 1024], P(('side', 'rep', 'tp')), may hold values from -6 to 6
- value_cache_slots: bfloat16 [512, 128, 1024], P(('side', 'rep', 'tp')), may hold values from -6 to 6
- cache_lengths: int32 [512], P(('side', 'rep', 'tp')), may hold values from 1 to 128, 8320 in all
Outputs:
- new_master: float32 [8192, 2048], P('tp', 'rep')
- new_first: bfloat16 [8192, 2048], P('tp', 'rep')
- new_second: bfloat16 [8192, 2048], P('tp', 'rep')
- attended: bfloat16 [512, 8192], P(('side', 'rep', 'tp'))
The draws below stay inside these ranges and needn't reach their ends.
Inputs may be any that keep to these rules, and one draw needn't show every extreme that they name: `cache_lengths`: the largest length is 128.
All inputs are finite; a program needn't handle non-finite values. No bound on the sum of `cache_lengths` on one device may be relied on, other than what follows from the above.
Results may differ from the reference program's by a relative error of at most 0.009.
Values may be sent and summed in bfloat16 or wider, within the bound.
No kernel may reach another device: no remote copies, remote signals or barrier semaphores. Data moves between devices by JAX's collectives and lax.ppermute only.
A program may use at most 64 MiB of HBM per device.

```python
import math
import jax
import jax.numpy as jnp
import numpy as np
from jax import lax

D = 8192
QUERY_HEADS = 64
KEY_VALUE_HEADS = 8
HEAD_SIZE = 128
ROWS_L = 1024
CACHE_SLOTS = 128
STEP = 10
KVD = 1024
KVW = 2048
LSIDES = 4
LEARN_ROWS = 32768
DECODE_ROWS = 512
N_REP = 8


def draw_queries(key, part):
    key = jax.random.fold_in(key, 5)
    decode_output = jax.random.normal(key, (DECODE_ROWS, QUERY_HEADS * HEAD_SIZE), jnp.float32)
    return jnp.clip(decode_output, -6.0, 6.0).astype(jnp.bfloat16)


def draw_key_cache_slots(key, part):
    key = jax.random.fold_in(key, 9)
    decode_output = jax.random.normal(key, (DECODE_ROWS, CACHE_SLOTS, KEY_VALUE_HEADS * HEAD_SIZE), jnp.float32)
    return jnp.clip(decode_output, -6.0, 6.0).astype(jnp.bfloat16)


def spiked(drawn, rng, source, target, parts, factor):
    def block_of(dim):
        return (jnp.arange(drawn.shape[dim]) // (drawn.shape[dim] // parts)).reshape((-1,) + (1,) * (drawn.ndim - 1 - dim))

    one_side = jax.random.permutation(rng, parts)[block_of(target)]
    other_side = (block_of(target) + parts // 2) % parts
    return jnp.where((block_of(source) == one_side) | (block_of(source) == other_side), factor * drawn, drawn)


def shard_levels(own_key, dims, pieces, low, largest):
    def one(axis_at, blocks):
        heights = jax.random.uniform(jax.random.fold_in(jax.random.fold_in(own_key, 6), axis_at), (blocks,), jnp.float32, low / len(pieces), largest / len(pieces))
        return jnp.repeat(jnp.exp(heights), dims[axis_at] // blocks).reshape((-1,) + (1,) * (len(dims) - axis_at - 1))

    gain = one(*pieces[0])
    for cut in pieces[1:]:
        gain = gain * one(*cut)
    return gain


def length_profile(count, total, most, lean):
    portions = [(1 << 20) // math.isqrt(standing ** lean) + 1 for standing in range(2, count + 1)]
    spare, holding = total - most - (count - 1), [1] * (count - 1)
    while spare > 0:
        free = [i for i in range(count - 1) if holding[i] < most]
        whole, left = sum([portions[i] for i in free]), spare
        for i in free:
            more = min(most - holding[i], max(1, left * portions[i] // whole), spare)
            holding[i] = holding[i] + more
            spare = spare - more
    return np.array([most] + holding)


def uneven(rng, amount, total, reach, slope):
    if amount == 2:
        one = jax.random.randint(rng, (), max(1, total - reach), min(reach, total - 1) + 1)
        return jnp.stack([one, total - one])
    lengths = jnp.asarray(length_profile(amount, total, reach, slope), jnp.int32)
    pairs = (amount - 1) // 2
    donor, receiver = lengths[1:1 + 2 * pairs:2], lengths[2:2 + 2 * pairs:2]
    margin = jnp.minimum(donor - 1, reach - receiver)
    moved = jax.random.randint(jax.random.fold_in(rng, 1), (pairs,), 0, 1 << 20) % (margin + 1)
    lengths = lengths.at[1:1 + 2 * pairs:2].set(donor - moved).at[2:2 + 2 * pairs:2].set(receiver + moved)
    return lengths[jax.random.permutation(jax.random.fold_in(rng, 2), amount)]


def normal_values(stream_key, shape, spread, bound, cuts=(), held_as=jnp.bfloat16):
    factor_of = shard_levels(stream_key, shape, cuts, -0.22, 0.18) if cuts else 1.0
    drawn = jax.random.normal(stream_key, shape, jnp.float32) * spread * factor_of
    return jnp.minimum(jnp.maximum(drawn, -bound), bound).astype(held_as)


def heavy_noise(stream_key, dims, scale, limit, cuts, heavy, kind=jnp.bfloat16):
    drawn = scale * jax.random.normal(stream_key, dims, jnp.float32)
    if cuts:
        drawn = drawn * shard_levels(stream_key, dims, cuts, -0.22, 0.18)
    return jnp.clip(spiked(drawn, jax.random.fold_in(stream_key, 3), *heavy), -limit, limit).astype(kind)


def setup_inputs(seed: int = 0) -> dict:
    arg_keys = jax.random.split(jax.random.key(seed), 11)
    learn_inputs = normal_values(arg_keys[0], (LSIDES, N_REP * ROWS_L, D), 1.0, 6.0, ((0, 4), (1, 8), (2, 16)))
    learn_grads = heavy_noise(arg_keys[1], (LSIDES, N_REP * ROWS_L, KVW), (LEARN_ROWS // 16) ** -0.5, 0.5, ((0, 4), (1, 128)), (1, 2, 128, 5.5))
    kv_master = normal_values(arg_keys[2], (D, KVW), D ** -0.5, 0.0625, ((0, 16), (1, 8)), jnp.float32)
    first_moment = normal_values(arg_keys[3], (D, KVW), 2.0, 12.0, ((0, 16), (1, 8)))
    second_moment = jnp.clip(jnp.exp(math.log(0.29882812) - 3.4024236 * jax.random.uniform(arg_keys[4], (D, KVW), jnp.float32) ** shard_levels(arg_keys[4], (D, KVW), ((0, 16), (1, 8)), -0.2, 0.2)), 0.0099487305, 0.29882812).astype(jnp.bfloat16)
    decode_inputs = normal_values(arg_keys[5], (DECODE_ROWS, D), 1.0, 6.0, ((0, 32), (1, 16)))
    queries = draw_queries(jax.random.fold_in(arg_keys[10], 71), 0)
    key_cache_slots = draw_key_cache_slots(jax.random.fold_in(arg_keys[10], 71), 0)
    value_cache_slots = normal_values(arg_keys[8], (DECODE_ROWS, CACHE_SLOTS, KVD), 1.0, 6.0, ((0, 512),))
    cache_lengths = uneven(arg_keys[9], DECODE_ROWS, DECODE_ROWS * CACHE_SLOTS // 8 + CACHE_SLOTS, CACHE_SLOTS, 1).astype(jnp.int32)
    return dict(learn_inputs=learn_inputs, learn_grads=learn_grads, kv_master=kv_master, first_moment=first_moment, second_moment=second_moment, decode_inputs=decode_inputs, queries=queries, key_cache_slots=key_cache_slots, value_cache_slots=value_cache_slots, cache_lengths=cache_lengths)


BETA_FIRST = 0.9
BETA_SECOND = 0.95
ADAM_EPSILON = 1e-08
LEARN_RATE = 0.001
DECAY_RATE = 0.1

def adamw(master, first_moment, second_moment, gradient):
    first_full = BETA_FIRST * first_moment.astype(jnp.float32) + (1.0 - BETA_FIRST) * gradient
    second_full = BETA_SECOND * second_moment.astype(jnp.float32) + (1.0 - BETA_SECOND) * gradient * gradient
    first_fix = 1.0 - BETA_FIRST ** STEP
    second_fix = 1.0 - BETA_SECOND ** STEP
    update = first_full / first_fix / (jnp.sqrt(second_full / second_fix) + ADAM_EPSILON)
    master_new = master - LEARN_RATE * (update + DECAY_RATE * master)
    return (master_new, first_full.astype(jnp.bfloat16), second_full.astype(jnp.bfloat16))

def attend(queries, key_cache_slots, value_cache_slots, cache_lengths, fresh_output):
    decode_row_count = queries.shape[0]
    slot_length = key_cache_slots.shape[1]
    query_groups = QUERY_HEADS // KEY_VALUE_HEADS
    query_head_rows = queries.astype(jnp.float32).reshape(decode_row_count, KEY_VALUE_HEADS, query_groups, HEAD_SIZE)
    stored_keys = key_cache_slots.astype(jnp.float32).reshape(decode_row_count, slot_length, KEY_VALUE_HEADS, HEAD_SIZE)
    stored_values = value_cache_slots.astype(jnp.float32).reshape(decode_row_count, slot_length, KEY_VALUE_HEADS, HEAD_SIZE)
    newest_keys = fresh_output[:, :KEY_VALUE_HEADS * HEAD_SIZE].astype(jnp.float32).reshape(decode_row_count, KEY_VALUE_HEADS, HEAD_SIZE)
    newest_values = fresh_output[:, KEY_VALUE_HEADS * HEAD_SIZE:].astype(jnp.float32).reshape(decode_row_count, KEY_VALUE_HEADS, HEAD_SIZE)
    score_scale = HEAD_SIZE ** (-0.5)
    scores = jnp.einsum('bkgd,blkd->bkgl', query_head_rows, stored_keys) * score_scale
    visible = jnp.arange(slot_length, dtype=jnp.int32)[None, :] < cache_lengths.astype(jnp.int32)[:, None]
    scores = jnp.where(visible[:, None, None, :], scores, -1e+30)
    self_score = jnp.einsum('zwai,zwi->zwa', query_head_rows, newest_keys) * score_scale
    highest = jnp.maximum(lax.optimization_barrier(jnp.max(scores, axis=-1)), self_score)
    weights = jnp.exp(scores - highest[..., None])
    own_weight = jnp.exp(self_score - highest)
    denominator = lax.optimization_barrier(jnp.sum(weights, axis=-1)) + own_weight
    probabilities = (weights / denominator[..., None]).astype(jnp.bfloat16)
    own_prob = (own_weight / denominator).astype(jnp.bfloat16)
    mixed = jnp.einsum('bkgl,blkd->bkgd', probabilities.astype(jnp.float32), stored_values)
    mixed = mixed + own_prob.astype(jnp.float32)[..., None] * newest_values[:, :, None, :]
    return mixed.reshape(decode_row_count, QUERY_HEADS * HEAD_SIZE).astype(jnp.bfloat16)

def reference(learn_inputs, learn_grads, kv_master, first_moment, second_moment, decode_inputs, queries, key_cache_slots, value_cache_slots, cache_lengths):

    def add_block(running, blocks):
        inputs_block, grads_block = blocks
        product = lax.dot_general(inputs_block.astype(jnp.float32), grads_block.astype(jnp.float32), (((0,), (0,)), ((), ())), precision=lax.Precision.HIGHEST)
        return (running + product, 0)
    initial = jnp.zeros((D, KVW), jnp.float32)
    gradient = lax.scan(add_block, initial, (learn_inputs, learn_grads))[0]
    master_new, first_new, second_new = adamw(kv_master, first_moment, second_moment, gradient)
    rounded_weights = master_new.astype(jnp.bfloat16)
    fresh_output = jnp.dot(decode_inputs, rounded_weights, preferred_element_type=jnp.float32).astype(jnp.bfloat16)
    attended = attend(queries, key_cache_slots, value_cache_slots, cache_lengths, fresh_output)
    return (master_new, first_new, second_new, attended)
```

```python
import jax
import jax.numpy as jnp
from jax import lax
from jax.sharding import Mesh
from jax.sharding import PartitionSpec as P

QUERY_HEADS = 64
KEY_VALUE_HEADS = 8
HEAD_SIZE = 128
STEP = 10


BETA_FIRST = 0.9
BETA_SECOND = 0.95
ADAM_EPSILON = 1e-08
LEARN_RATE = 0.001
DECAY_RATE = 0.1


def adamw(master, first_moment, second_moment, gradient):
    first_full = BETA_FIRST * first_moment.astype(jnp.float32) + (1.0 - BETA_FIRST) * gradient
    second_full = (
        BETA_SECOND * second_moment.astype(jnp.float32) + (1.0 - BETA_SECOND) * gradient * gradient
    )
    first_fix = 1.0 - BETA_FIRST**STEP
    second_fix = 1.0 - BETA_SECOND**STEP
    update = first_full / first_fix / (jnp.sqrt(second_full / second_fix) + ADAM_EPSILON)
    master_new = master - LEARN_RATE * (update + DECAY_RATE * master)
    return (master_new, first_full.astype(jnp.bfloat16), second_full.astype(jnp.bfloat16))


def attend(queries, key_cache_slots, value_cache_slots, cache_lengths, fresh_output):
    decode_row_count = queries.shape[0]
    slot_length = key_cache_slots.shape[1]
    query_groups = QUERY_HEADS // KEY_VALUE_HEADS
    query_head_rows = queries.reshape(decode_row_count, KEY_VALUE_HEADS, query_groups, HEAD_SIZE)
    stored_keys = key_cache_slots.reshape(decode_row_count, slot_length, KEY_VALUE_HEADS, HEAD_SIZE)
    stored_values = value_cache_slots.reshape(
        decode_row_count, slot_length, KEY_VALUE_HEADS, HEAD_SIZE
    )
    newest_keys = fresh_output[:, : KEY_VALUE_HEADS * HEAD_SIZE].reshape(
        decode_row_count, KEY_VALUE_HEADS, HEAD_SIZE
    )
    newest_values = fresh_output[:, KEY_VALUE_HEADS * HEAD_SIZE :].reshape(
        decode_row_count, KEY_VALUE_HEADS, HEAD_SIZE
    )
    score_scale = HEAD_SIZE ** (-0.5)
    scores = (
        jnp.einsum(
            "bkgd,blkd->bkgl", query_head_rows, stored_keys, preferred_element_type=jnp.float32
        )
        * score_scale
    )
    visible = jnp.arange(slot_length, dtype=jnp.int32)[None, :] < cache_lengths[:, None]
    scores = jnp.where(visible[:, None, None, :], scores, -1e30)
    self_score = (
        jnp.einsum(
            "zwai,zwi->zwa", query_head_rows, newest_keys, preferred_element_type=jnp.float32
        )
        * score_scale
    )
    highest = jnp.maximum(jnp.max(scores, axis=-1), self_score)
    weights = jnp.exp(scores - highest[..., None])
    own_weight = jnp.exp(self_score - highest)
    denominator = jnp.sum(weights, axis=-1) + own_weight
    probabilities = (weights / denominator[..., None]).astype(jnp.bfloat16)
    own_prob = (own_weight / denominator).astype(jnp.bfloat16)
    mixed = jnp.einsum(
        "bkgl,blkd->bkgd", probabilities, stored_values, preferred_element_type=jnp.float32
    )
    mixed = (
        mixed
        + own_prob.astype(jnp.float32)[..., None] * newest_values.astype(jnp.float32)[:, :, None, :]
    )
    return mixed.reshape(decode_row_count, QUERY_HEADS * HEAD_SIZE).astype(jnp.bfloat16)


FINE_AXES = ("side", "x", "core", "zhi", "y")
REP = ("x", "core")
TP = ("zhi", "y")


def pick_core(columns, core):
    return lax.dynamic_index_in_dim(columns, core, axis=2, keepdims=False)


def gather_cotangents(pieces):
    pairs = lax.all_gather(pieces, "zhi", axis=1)
    return lax.all_gather(pairs, "y", axis=2)


def local(
    learn_inputs,
    learn_grads,
    kv_master,
    first_moment,
    second_moment,
    decode_inputs,
    queries,
    key_cache_slots,
    value_cache_slots,
    cache_lengths,
):
    core = lax.axis_index("core")
    swap = [(0, 1), (1, 0)]
    inputs_own = learn_inputs[0]
    row_count, feature_count = inputs_own.shape
    x_count, side_count = lax.axis_size("x"), lax.axis_size("side")
    block_width = kv_master.shape[1]
    columns = learn_grads[0].reshape(-1, x_count, 2, block_width)
    grads_other = lax.ppermute(pick_core(columns, 1 - core), "core", swap)
    pieces = jnp.stack([pick_core(columns, core), grads_other])
    inputs_other = lax.ppermute(inputs_own, "core", swap)
    gathered = gather_cotangents(pieces)
    grads_all = gathered.reshape(2, row_count, x_count, block_width)
    inputs_all = jnp.stack([inputs_own, inputs_other])
    partial = jnp.einsum(
        "prf,prxc->xfc", inputs_all, grads_all, preferred_element_type=jnp.float32
    ).astype(jnp.bfloat16)
    quarter = feature_count // side_count
    partial = partial.reshape(x_count * side_count, quarter, block_width)
    terms = lax.all_to_all(partial, ("x", "side"), 0, 0, tiled=True)
    own_quarter = jnp.sum(terms.astype(jnp.float32), axis=0).astype(jnp.bfloat16)
    spread = jnp.broadcast_to(own_quarter[None], (side_count, quarter, block_width))
    gradient = lax.all_to_all(spread, "side", 0, 0, tiled=True)
    gradient = gradient.reshape(feature_count, block_width).astype(jnp.float32)
    master_new, first_new, second_new = adamw(kv_master, first_moment, second_moment, gradient)
    rounded_weights = master_new.astype(jnp.bfloat16)
    decode_rows = lax.all_gather(decode_inputs, REP, axis=0, tiled=True)
    partial_fresh = jnp.dot(decode_rows, rounded_weights, preferred_element_type=jnp.float32)
    rep_count, tp_count = lax.axis_size(REP), lax.axis_size(TP)
    partial_fresh = partial_fresh.reshape(rep_count, tp_count, block_width)
    fresh_terms = lax.all_to_all(partial_fresh, TP, 1, 1, tiled=True)
    fresh_block = jnp.sum(fresh_terms, axis=1).astype(jnp.bfloat16)
    fresh_output = lax.all_to_all(fresh_block, REP, 0, 0, tiled=True).reshape(1, -1)
    attended = attend(queries, key_cache_slots, value_cache_slots, cache_lengths, fresh_output)
    return (master_new, first_new, second_new, attended)


def solution(mesh):
    fine = Mesh(mesh.devices.reshape(mesh.devices.shape[0], -1, 2, 2, 8), FINE_AXES)
    placed = (
        P("side", REP, TP),
        P("side", REP + TP, None),
        P(TP, REP),
        P(TP, REP),
        P(TP, REP),
        P(("side",) + REP, TP),
        P(("side",) + REP + TP, None),
        P(("side",) + REP + TP, None, None),
        P(("side",) + REP + TP, None, None),
        P(("side",) + REP + TP),
    )
    return jax.shard_map(
        local,
        mesh=fine,
        in_specs=placed,
        out_specs=(P(TP, REP), P(TP, REP), P(TP, REP), P(("side",) + REP + TP, None)),
        check_vma=False,
    )
```

```python
import jax
import jax.numpy as jnp
from jax import lax
from jax.sharding import Mesh
from jax.sharding import PartitionSpec as P

QUERY_HEADS = 64
KEY_VALUE_HEADS = 8
HEAD_SIZE = 128
STEP = 10


BETA_FIRST = 0.9
BETA_SECOND = 0.95
ADAM_EPSILON = 1e-08
LEARN_RATE = 0.001
DECAY_RATE = 0.1


def adamw(master, first_moment, second_moment, gradient):
    first_full = BETA_FIRST * first_moment.astype(jnp.float32) + (1.0 - BETA_FIRST) * gradient
    second_full = (
        BETA_SECOND * second_moment.astype(jnp.float32) + (1.0 - BETA_SECOND) * gradient * gradient
    )
    first_fix = 1.0 - BETA_FIRST**STEP
    second_fix = 1.0 - BETA_SECOND**STEP
    update = first_full / first_fix / (jnp.sqrt(second_full / second_fix) + ADAM_EPSILON)
    master_new = master - LEARN_RATE * (update + DECAY_RATE * master)
    return (master_new, first_full.astype(jnp.bfloat16), second_full.astype(jnp.bfloat16))


def attend(queries, key_cache_slots, value_cache_slots, cache_lengths, fresh_output):
    decode_row_count = queries.shape[0]
    slot_length = key_cache_slots.shape[1]
    query_groups = QUERY_HEADS // KEY_VALUE_HEADS
    query_head_rows = queries.reshape(decode_row_count, KEY_VALUE_HEADS, query_groups, HEAD_SIZE)
    stored_keys = key_cache_slots.reshape(decode_row_count, slot_length, KEY_VALUE_HEADS, HEAD_SIZE)
    stored_values = value_cache_slots.reshape(
        decode_row_count, slot_length, KEY_VALUE_HEADS, HEAD_SIZE
    )
    newest_keys = fresh_output[:, : KEY_VALUE_HEADS * HEAD_SIZE].reshape(
        decode_row_count, KEY_VALUE_HEADS, HEAD_SIZE
    )
    newest_values = fresh_output[:, KEY_VALUE_HEADS * HEAD_SIZE :].reshape(
        decode_row_count, KEY_VALUE_HEADS, HEAD_SIZE
    )
    score_scale = HEAD_SIZE ** (-0.5)
    scores = (
        jnp.einsum(
            "bkgd,blkd->bkgl", query_head_rows, stored_keys, preferred_element_type=jnp.float32
        )
        * score_scale
    )
    visible = jnp.arange(slot_length, dtype=jnp.int32)[None, :] < cache_lengths[:, None]
    scores = jnp.where(visible[:, None, None, :], scores, -1e30)
    self_score = (
        jnp.einsum(
            "zwai,zwi->zwa", query_head_rows, newest_keys, preferred_element_type=jnp.float32
        )
        * score_scale
    )
    highest = jnp.maximum(jnp.max(scores, axis=-1), self_score)
    weights = jnp.exp(scores - highest[..., None])
    own_weight = jnp.exp(self_score - highest)
    denominator = jnp.sum(weights, axis=-1) + own_weight
    probabilities = (weights / denominator[..., None]).astype(jnp.bfloat16)
    own_prob = (own_weight / denominator).astype(jnp.bfloat16)
    mixed = jnp.einsum(
        "bkgl,blkd->bkgd", probabilities, stored_values, preferred_element_type=jnp.float32
    )
    mixed = (
        mixed
        + own_prob.astype(jnp.float32)[..., None] * newest_values.astype(jnp.float32)[:, :, None, :]
    )
    return mixed.reshape(decode_row_count, QUERY_HEADS * HEAD_SIZE).astype(jnp.bfloat16)


FINE_AXES = ("side", "x", "core", "zhi", "y")
REP = ("x", "core")
TP = ("zhi", "y")
CHUNKS = 2


def swap_over(array, axis):
    return lax.ppermute(array, axis, [(0, 1), (1, 0)])


def other_features(inputs_own):
    half = lax.axis_index("zhi")
    halves = inputs_own.reshape(2, -1, inputs_own.shape[1])
    kept = lax.dynamic_index_in_dim(halves, half, 0, keepdims=False)
    received = swap_over(lax.dynamic_index_in_dim(halves, 1 - half, 0, keepdims=False), "zhi")
    return kept, received


def ordered(kept, received, axis):
    first = lax.axis_index("zhi") == 0
    return jnp.stack([jnp.where(first, kept, received), jnp.where(first, received, kept)], axis)


def summed(terms):
    return jnp.sum(terms.astype(jnp.float32), axis=0).astype(jnp.bfloat16)


def local(
    learn_inputs,
    learn_grads,
    kv_master,
    first_moment,
    second_moment,
    decode_inputs,
    queries,
    key_cache_slots,
    value_cache_slots,
    cache_lengths,
):
    core = lax.axis_index("core")
    inputs_own = learn_inputs[0]
    feature_count = inputs_own.shape[1]
    x_count, side_count = lax.axis_size("x"), lax.axis_size("side")
    block_width = kv_master.shape[1]
    chunk_width = block_width // CHUNKS
    quarter = feature_count // side_count

    columns = learn_grads[0].reshape(-1, x_count, 2, CHUNKS, chunk_width)
    grads_other = swap_over(
        lax.dynamic_index_in_dim(columns, 1 - core, axis=2, keepdims=False), "core"
    )
    grads_own = lax.dynamic_index_in_dim(columns, core, axis=2, keepdims=False)
    kept, received = other_features(inputs_own)
    kept_pair = jnp.stack([kept, swap_over(kept, "core")])
    received_pair = jnp.stack([received, swap_over(received, "core")])
    inputs_all = ordered(kept_pair, received_pair, 2)
    decode_rows = lax.all_gather(decode_inputs, REP, axis=0, tiled=True)
    inputs_all, decode_rows = lax.optimization_barrier((inputs_all, decode_rows))

    gradients = []
    for chunk in range(CHUNKS):
        piece = jnp.stack([grads_own[:, :, chunk], grads_other[:, :, chunk]])
        grads_all = lax.all_gather(piece, "y", axis=1, tiled=True)
        partial = jnp.einsum(
            "prhf,prxn->xhfn", inputs_all, grads_all, preferred_element_type=jnp.float32
        ).astype(jnp.bfloat16)
        partial = partial.reshape(x_count, 2 * feature_count, chunk_width)
        over_x = summed(lax.all_to_all(partial, "x", 0, 0, tiled=True))
        over_x = over_x.reshape(2 * side_count, quarter, chunk_width)
        own_quarter = summed(lax.all_to_all(over_x, ("zhi", "side"), 0, 0, tiled=True))
        spread = jnp.broadcast_to(own_quarter[None], (side_count, quarter, chunk_width))
        gradients.append(lax.all_to_all(spread, "side", 0, 0, tiled=True).reshape(feature_count, chunk_width))
    gradient = jnp.concatenate(gradients, axis=1).astype(jnp.float32)
    master_new, first_new, second_new = adamw(kv_master, first_moment, second_moment, gradient)
    rounded_weights = master_new.astype(jnp.bfloat16)
    partial_fresh = jnp.dot(decode_rows, rounded_weights, preferred_element_type=jnp.float32)
    partial_fresh = partial_fresh.astype(jnp.bfloat16).reshape(-1, 2, block_width // 2)
    fresh_terms = lax.all_to_all(partial_fresh, REP + TP, 0, 0, tiled=True)
    fresh_terms = fresh_terms.reshape(lax.axis_size(REP), lax.axis_size(TP), block_width)
    fresh_output = jnp.sum(fresh_terms.astype(jnp.float32), axis=1).astype(jnp.bfloat16)
    fresh_output = fresh_output.reshape(1, -1)
    attended = attend(queries, key_cache_slots, value_cache_slots, cache_lengths, fresh_output)
    return (master_new, first_new, second_new, attended)


def solution(mesh):
    fine = Mesh(mesh.devices.reshape(mesh.devices.shape[0], -1, 2, 2, 8), FINE_AXES)
    placed = (
        P("side", REP, TP),
        P("side", REP + TP, None),
        P(TP, REP),
        P(TP, REP),
        P(TP, REP),
        P(("side",) + REP, TP),
        P(("side",) + REP + TP, None),
        P(("side",) + REP + TP, None, None),
        P(("side",) + REP + TP, None, None),
        P(("side",) + REP + TP),
    )
    return jax.shard_map(
        local,
        mesh=fine,
        in_specs=placed,
        out_specs=(P(TP, REP), P(TP, REP), P(TP, REP), P(("side",) + REP + TP, None)),
        check_vma=False,
    )
```

```python
import jax
import jax.numpy as jnp
from jax import lax
from jax.experimental import pallas as pl
from jax.experimental.pallas import tpu as pltpu
from jax.sharding import Mesh
from jax.sharding import PartitionSpec as P

QUERY_HEADS = 64
KEY_VALUE_HEADS = 8
HEAD_SIZE = 128
STEP = 10


BETA_FIRST = 0.9
BETA_SECOND = 0.95
ADAM_EPSILON = 1e-08
LEARN_RATE = 0.001
DECAY_RATE = 0.1


def adamw(master, first_moment, second_moment, gradient):
    first_full = BETA_FIRST * first_moment.astype(jnp.float32) + (1.0 - BETA_FIRST) * gradient
    second_full = (
        BETA_SECOND * second_moment.astype(jnp.float32) + (1.0 - BETA_SECOND) * gradient * gradient
    )
    first_fix = 1.0 - BETA_FIRST**STEP
    second_fix = 1.0 - BETA_SECOND**STEP
    update = first_full / first_fix / (jnp.sqrt(second_full / second_fix) + ADAM_EPSILON)
    master_new = master - LEARN_RATE * (update + DECAY_RATE * master)
    return (master_new, first_full.astype(jnp.bfloat16), second_full.astype(jnp.bfloat16))


def attend(queries, key_cache_slots, value_cache_slots, cache_lengths, fresh_output):
    decode_row_count = queries.shape[0]
    slot_length = key_cache_slots.shape[1]
    query_groups = QUERY_HEADS // KEY_VALUE_HEADS
    query_head_rows = queries.reshape(decode_row_count, KEY_VALUE_HEADS, query_groups, HEAD_SIZE)
    stored_keys = key_cache_slots.reshape(decode_row_count, slot_length, KEY_VALUE_HEADS, HEAD_SIZE)
    stored_values = value_cache_slots.reshape(
        decode_row_count, slot_length, KEY_VALUE_HEADS, HEAD_SIZE
    )
    newest_keys = fresh_output[:, : KEY_VALUE_HEADS * HEAD_SIZE].reshape(
        decode_row_count, KEY_VALUE_HEADS, HEAD_SIZE
    )
    newest_values = fresh_output[:, KEY_VALUE_HEADS * HEAD_SIZE :].reshape(
        decode_row_count, KEY_VALUE_HEADS, HEAD_SIZE
    )
    score_scale = HEAD_SIZE ** (-0.5)
    scores = (
        jnp.einsum(
            "bkgd,blkd->bkgl", query_head_rows, stored_keys, preferred_element_type=jnp.float32
        )
        * score_scale
    )
    visible = jnp.arange(slot_length, dtype=jnp.int32)[None, :] < cache_lengths[:, None]
    scores = jnp.where(visible[:, None, None, :], scores, -1e30)
    self_score = (
        jnp.einsum(
            "zwai,zwi->zwa", query_head_rows, newest_keys, preferred_element_type=jnp.float32
        )
        * score_scale
    )
    highest = jnp.maximum(jnp.max(scores, axis=-1), self_score)
    weights = jnp.exp(scores - highest[..., None])
    own_weight = jnp.exp(self_score - highest)
    denominator = jnp.sum(weights, axis=-1) + own_weight
    probabilities = (weights / denominator[..., None]).astype(jnp.bfloat16)
    own_prob = (own_weight / denominator).astype(jnp.bfloat16)
    mixed = jnp.einsum(
        "bkgl,blkd->bkgd", probabilities, stored_values, preferred_element_type=jnp.float32
    )
    mixed = (
        mixed
        + own_prob.astype(jnp.float32)[..., None] * newest_values.astype(jnp.float32)[:, :, None, :]
    )
    return mixed.reshape(decode_row_count, QUERY_HEADS * HEAD_SIZE).astype(jnp.bfloat16)


FINE_AXES = ("side", "x", "core", "zhi", "y")
REP = ("x", "core")
TP = ("zhi", "y")


def swap_over(array, axis):
    return lax.ppermute(array, axis, [(0, 1), (1, 0)])


def shifted(array, axis, by):
    count = lax.axis_size(axis)
    return lax.ppermute(array, axis, [(i, (i + by) % count) for i in range(count)])


def gathered_round(piece):
    half = piece.shape[0] // 2
    behind1, ahead1 = shifted(piece, "y", 1), shifted(piece, "y", -1)
    behind2, ahead2 = shifted(piece, "y", 2), shifted(piece, "y", -2)
    behind3, ahead3 = shifted(behind2, "y", 1), shifted(ahead2, "y", -1)
    across = [shifted(behind3[:half], "y", 1), shifted(ahead3[half:], "y", -1)]
    return [piece, behind1, behind2, behind3, *across, ahead3, ahead2, ahead1]


def own_columns(columns, width, core):
    blocks = [columns[:, i : i + width] for i in range(0, columns.shape[1], width)]
    even, odd = jnp.concatenate(blocks[::2], axis=1), jnp.concatenate(blocks[1::2], axis=1)
    return jnp.where(core == 0, even, odd), jnp.where(core == 0, odd, even)


def product_kernel(position, inputs, kept_other, received_own, received_other, *refs):
    *pieces, out = refs
    half, along = position[0], position[1]
    count = lax.axis_size("y")
    feature_count = inputs.shape[1]
    rows = received_own.shape[0] // count
    x_count, _, width = out.shape
    starts = [
        pl.multiple_of(lax.rem(along - behind + count, count) * rows, rows)
        for behind in range(count)
    ]
    half_start = pl.multiple_of(half * received_own.shape[0], rows)
    sides = (
        (inputs, half_start, kept_other, half),
        (received_own, 0, received_other, 1 - half),
    )
    for own, offset, other, place in sides:
        left = jnp.concatenate(
            [
                block
                for start in starts
                for block in (own[pl.ds(offset + start, rows), :], other[pl.ds(start, rows), :])
            ]
        )
        target = pl.ds(pl.multiple_of(place * feature_count, feature_count), feature_count)
        for x in range(x_count):
            right = jnp.concatenate([piece[:, x * width : (x + 1) * width] for piece in pieces])
            out[x, target, :] = lax.dot_general(
                left, right, (((0,), (0,)), ((), ())), preferred_element_type=jnp.float32
            ).astype(out.dtype)


def products(half, inputs, kept_other, received_own, received_other, pieces, x_count):
    feature_count = inputs.shape[1]
    width = pieces[0].shape[1] // x_count
    position = jnp.stack([half, lax.axis_index("y")]).astype(jnp.int32)
    operands = (inputs, kept_other, received_own, received_other, *pieces)
    out_shape = jax.ShapeDtypeStruct((x_count, 2 * feature_count, width), jnp.bfloat16)
    return pl.pallas_call(
        product_kernel,
        out_shape=out_shape,
        in_specs=[pl.BlockSpec(memory_space=pltpu.SMEM)]
        + [pl.BlockSpec(memory_space=pltpu.VMEM)] * len(operands),
        out_specs=pl.BlockSpec(memory_space=pltpu.VMEM),
        compiler_params=pltpu.CompilerParams(vmem_limit_bytes=24 * 2**20),
        cost_estimate=pl.CostEstimate(
            flops=4 * feature_count * received_own.shape[0] * 2 * x_count * width,
            bytes_accessed=8 * 2**20,
            transcendentals=0,
        ),
        name="products",
    )(position, *operands)


def summed(terms):
    return jnp.sum(terms.astype(jnp.float32), axis=0).astype(jnp.bfloat16)


def local(
    learn_inputs,
    learn_grads,
    kv_master,
    first_moment,
    second_moment,
    decode_inputs,
    queries,
    key_cache_slots,
    value_cache_slots,
    cache_lengths,
):
    core, half = lax.axis_index("core"), lax.axis_index("zhi")
    x_count, side_count = lax.axis_size("x"), lax.axis_size("side")
    feature_count = learn_inputs.shape[2]
    block_width = kv_master.shape[1]
    quarter = feature_count // side_count

    grads_own, grads_sent = own_columns(learn_grads[0], block_width, core)
    piece = jnp.concatenate([grads_own, swap_over(grads_sent, "core")])
    pieces = gathered_round(piece)

    inputs = learn_inputs[0]
    row_halves = inputs.reshape(2, -1, feature_count)
    kept = lax.dynamic_index_in_dim(row_halves, half, 0, keepdims=False)
    received = swap_over(lax.dynamic_index_in_dim(row_halves, 1 - half, 0, keepdims=False), "zhi")
    kept_other, received_other = swap_over(kept, "core"), swap_over(received, "core")
    decode_rows = lax.all_gather(decode_inputs, REP, axis=0, tiled=True)
    received_other, decode_rows = lax.optimization_barrier((received_other, decode_rows))

    partial = products(half, inputs, kept_other, received, received_other, pieces, x_count)
    over_x = summed(lax.all_to_all(partial, "x", 0, 0, tiled=True))
    over_x = over_x.reshape(2 * side_count, quarter, block_width)
    own_quarter = summed(lax.all_to_all(over_x, ("zhi", "side"), 0, 0, tiled=True))
    spread = jnp.broadcast_to(own_quarter[None], (side_count, quarter, block_width))
    gradient = lax.all_to_all(spread, "side", 0, 0, tiled=True)
    gradient = gradient.reshape(feature_count, block_width).astype(jnp.float32)
    master_new, first_new, second_new = adamw(kv_master, first_moment, second_moment, gradient)
    rounded_weights = master_new.astype(jnp.bfloat16)
    partial_fresh = jnp.dot(decode_rows, rounded_weights, preferred_element_type=jnp.float32)
    partial_fresh = partial_fresh.astype(jnp.bfloat16).reshape(-1, 2, block_width // 2)
    fresh_terms = lax.all_to_all(partial_fresh, REP + TP, 0, 0, tiled=True)
    fresh_terms = fresh_terms.reshape(lax.axis_size(REP), lax.axis_size(TP), block_width)
    fresh_output = jnp.sum(fresh_terms.astype(jnp.float32), axis=1).astype(jnp.bfloat16)
    fresh_output = fresh_output.reshape(1, -1)
    attended = attend(queries, key_cache_slots, value_cache_slots, cache_lengths, fresh_output)
    return (master_new, first_new, second_new, attended)


def solution(mesh):
    fine = Mesh(mesh.devices.reshape(mesh.devices.shape[0], -1, 2, 2, 8), FINE_AXES)
    placed = (
        P("side", REP, TP),
        P("side", REP + TP, None),
        P(TP, REP),
        P(TP, REP),
        P(TP, REP),
        P(("side",) + REP, TP),
        P(("side",) + REP + TP, None),
        P(("side",) + REP + TP, None, None),
        P(("side",) + REP + TP, None, None),
        P(("side",) + REP + TP),
    )
    return jax.shard_map(
        local,
        mesh=fine,
        in_specs=placed,
        out_specs=(P(TP, REP), P(TP, REP), P(TP, REP), P(("side",) + REP + TP, None)),
        check_vma=False,
    )
```

```python
import jax
import jax.numpy as jnp
from jax import lax
from jax.experimental import pallas as pl
from jax.experimental.pallas import tpu as pltpu
from jax.sharding import Mesh
from jax.sharding import PartitionSpec as P

QUERY_HEADS = 64
KEY_VALUE_HEADS = 8
HEAD_SIZE = 128
STEP = 10


BETA_FIRST = 0.9
BETA_SECOND = 0.95
ADAM_EPSILON = 1e-08
LEARN_RATE = 0.001
DECAY_RATE = 0.1


def adamw(master, first_moment, second_moment, gradient):
    first_full = BETA_FIRST * first_moment.astype(jnp.float32) + (1.0 - BETA_FIRST) * gradient
    second_full = (
        BETA_SECOND * second_moment.astype(jnp.float32) + (1.0 - BETA_SECOND) * gradient * gradient
    )
    first_fix = 1.0 - BETA_FIRST**STEP
    second_fix = 1.0 - BETA_SECOND**STEP
    update = first_full / first_fix / (jnp.sqrt(second_full / second_fix) + ADAM_EPSILON)
    master_new = master - LEARN_RATE * (update + DECAY_RATE * master)
    return (master_new, first_full.astype(jnp.bfloat16), second_full.astype(jnp.bfloat16))


def attend(queries, key_cache_slots, value_cache_slots, cache_lengths, fresh_output):
    decode_row_count = queries.shape[0]
    slot_length = key_cache_slots.shape[1]
    query_groups = QUERY_HEADS // KEY_VALUE_HEADS
    query_head_rows = queries.reshape(decode_row_count, KEY_VALUE_HEADS, query_groups, HEAD_SIZE)
    stored_keys = key_cache_slots.reshape(decode_row_count, slot_length, KEY_VALUE_HEADS, HEAD_SIZE)
    stored_values = value_cache_slots.reshape(
        decode_row_count, slot_length, KEY_VALUE_HEADS, HEAD_SIZE
    )
    newest_keys = fresh_output[:, : KEY_VALUE_HEADS * HEAD_SIZE].reshape(
        decode_row_count, KEY_VALUE_HEADS, HEAD_SIZE
    )
    newest_values = fresh_output[:, KEY_VALUE_HEADS * HEAD_SIZE :].reshape(
        decode_row_count, KEY_VALUE_HEADS, HEAD_SIZE
    )
    score_scale = HEAD_SIZE ** (-0.5)
    scores = (
        jnp.einsum(
            "bkgd,blkd->bkgl", query_head_rows, stored_keys, preferred_element_type=jnp.float32
        )
        * score_scale
    )
    visible = jnp.arange(slot_length, dtype=jnp.int32)[None, :] < cache_lengths[:, None]
    scores = jnp.where(visible[:, None, None, :], scores, -1e30)
    self_score = (
        jnp.einsum(
            "zwai,zwi->zwa", query_head_rows, newest_keys, preferred_element_type=jnp.float32
        )
        * score_scale
    )
    highest = jnp.maximum(jnp.max(scores, axis=-1), self_score)
    weights = jnp.exp(scores - highest[..., None])
    own_weight = jnp.exp(self_score - highest)
    denominator = jnp.sum(weights, axis=-1) + own_weight
    probabilities = (weights / denominator[..., None]).astype(jnp.bfloat16)
    own_prob = (own_weight / denominator).astype(jnp.bfloat16)
    mixed = jnp.einsum(
        "bkgl,blkd->bkgd", probabilities, stored_values, preferred_element_type=jnp.float32
    )
    mixed = (
        mixed
        + own_prob.astype(jnp.float32)[..., None] * newest_values.astype(jnp.float32)[:, :, None, :]
    )
    return mixed.reshape(decode_row_count, QUERY_HEADS * HEAD_SIZE).astype(jnp.bfloat16)


FINE_AXES = ("side", "x", "core", "zhi", "y")
REP = ("x", "core")
TP = ("zhi", "y")


def swap_over(array, axis):
    return lax.ppermute(array, axis, [(0, 1), (1, 0)])


def shifted(array, axis, by):
    count = lax.axis_size(axis)
    return lax.ppermute(array, axis, [(i, (i + by) % count) for i in range(count)])


def gathered_round(piece, inputs_sent):
    half = piece.shape[0] // 2
    piece, inputs_sent = lax.optimization_barrier((piece, inputs_sent))
    received = swap_over(inputs_sent, "zhi")
    behind1, ahead1 = shifted(piece, "y", 1), shifted(piece, "y", -1)
    behind2, ahead2 = shifted(piece, "y", 2), shifted(piece, "y", -2)
    behind3, ahead3 = shifted(behind2, "y", 1), shifted(ahead2, "y", -1)
    behind3, ahead3, received = lax.optimization_barrier((behind3, ahead3, received))
    across = [shifted(behind3[:half], "y", 1), shifted(ahead3[half:], "y", -1)]
    return [piece, behind1, behind2, behind3, *across, ahead3, ahead2, ahead1], received


def own_columns(columns, width, core):
    blocks = [columns[:, i : i + width] for i in range(0, columns.shape[1], width)]
    even, odd = jnp.concatenate(blocks[::2], axis=1), jnp.concatenate(blocks[1::2], axis=1)
    return jnp.where(core == 0, even, odd), jnp.where(core == 0, odd, even)


def product_kernel(position, inputs, received, others, decode_own, *refs):
    *pieces, out = refs
    half, along, core = position[0], position[1], position[2]
    count = lax.axis_size("y")
    feature_count = inputs.shape[1]
    half_rows = received.shape[0]
    rows = half_rows // count
    x_count, _, width = out.shape
    starts = [
        pl.multiple_of(lax.rem(along - behind + count, count) * rows, rows)
        for behind in range(count)
    ]
    half_start = pl.multiple_of(half * half_rows, half_rows)
    for own, offset, other_offset, place in (
        (inputs, half_start, 0, half),
        (received, 0, half_rows, 1 - half),
    ):
        left = jnp.concatenate(
            [
                block
                for start in starts
                for block in (
                    own[pl.ds(offset + start, rows), :],
                    others[pl.ds(other_offset + start, rows), :],
                )
            ]
        )
        target = pl.ds(pl.multiple_of(place * feature_count, feature_count), feature_count)
        for x in range(x_count):
            right = jnp.concatenate([piece[:, x * width : (x + 1) * width] for piece in pieces])
            out[x, target, :] = lax.dot_general(
                left, right, (((0,), (0,)), ((), ())), preferred_element_type=jnp.float32
            ).astype(out.dtype)
    decode_rows, decode_parts = decode_own.shape[0], feature_count // width
    for rows_of_core, place in (
        (decode_own[...], core),
        (others[2 * half_rows :, :], 1 - core),
    ):
        for part in range(decode_parts):
            start = 2 * feature_count + (place * decode_parts + part) * decode_rows
            target = pl.ds(pl.multiple_of(start, decode_rows), decode_rows)
            for x in range(x_count):
                out[x, target, :] = rows_of_core[:, part * width : (part + 1) * width]


def products(inputs, received, others, decode_own, pieces, x_count):
    feature_count = inputs.shape[1]
    width = pieces[0].shape[1] // x_count
    position = jnp.stack([lax.axis_index(axis) for axis in ("zhi", "y", "core")]).astype(jnp.int32)
    operands = (inputs, received, others, decode_own, *pieces)
    extra_rows = 2 * decode_own.size // width
    out_shape = jax.ShapeDtypeStruct(
        (x_count, 2 * feature_count + extra_rows, width), jnp.bfloat16
    )
    return pl.pallas_call(
        product_kernel,
        out_shape=out_shape,
        in_specs=[pl.BlockSpec(memory_space=pltpu.SMEM)]
        + [pl.BlockSpec(memory_space=pltpu.VMEM)] * len(operands),
        out_specs=pl.BlockSpec(memory_space=pltpu.VMEM),
        compiler_params=pltpu.CompilerParams(vmem_limit_bytes=24 * 2**20),
        cost_estimate=pl.CostEstimate(
            flops=8 * feature_count * received.shape[0] * x_count * width,
            bytes_accessed=8 * 2**20,
            transcendentals=0,
        ),
        name="products",
    )(position, *operands)


def summed(terms):
    return jnp.sum(terms.astype(jnp.float32), axis=0).astype(jnp.bfloat16)


def local(
    learn_inputs,
    learn_grads,
    kv_master,
    first_moment,
    second_moment,
    decode_inputs,
    queries,
    key_cache_slots,
    value_cache_slots,
    cache_lengths,
):
    core, half = lax.axis_index("core"), lax.axis_index("zhi")
    x_count, side_count = lax.axis_size("x"), lax.axis_size("side")
    feature_count = learn_inputs.shape[2]
    block_width = kv_master.shape[1]
    quarter = feature_count // side_count

    grads_own, grads_sent = own_columns(learn_grads[0], block_width, core)
    piece = jnp.concatenate([grads_own, swap_over(grads_sent, "core")])

    inputs = learn_inputs[0]
    row_halves = inputs.reshape(2, -1, feature_count)
    kept = jnp.where(half == 0, row_halves[0], row_halves[1])
    inputs_sent = jnp.where(half == 0, row_halves[1], row_halves[0])
    pieces, received = gathered_round(piece, inputs_sent)
    others = swap_over(jnp.concatenate([kept, received, decode_inputs]), "core")

    partial = products(inputs, received, others, decode_inputs, pieces, x_count)
    terms = lax.all_to_all(partial, "x", 0, 0, tiled=True)
    over_x = summed(terms[:, : 2 * feature_count])
    over_x = over_x.reshape(2 * side_count, quarter, block_width)
    decode_rows = terms[:, 2 * feature_count :].reshape(
        x_count, 2, feature_count // block_width, -1, block_width
    )
    decode_rows = decode_rows.transpose(0, 1, 3, 2, 4).reshape(-1, feature_count)
    own_quarter = summed(lax.all_to_all(over_x, ("zhi", "side"), 0, 0, tiled=True))
    spread = jnp.broadcast_to(own_quarter[None], (side_count, quarter, block_width))
    gradient = lax.all_to_all(spread, "side", 0, 0, tiled=True)
    gradient = gradient.reshape(feature_count, block_width).astype(jnp.float32)
    master_new, first_new, second_new = adamw(kv_master, first_moment, second_moment, gradient)
    rounded_weights = master_new.astype(jnp.bfloat16)
    partial_fresh = jnp.dot(decode_rows, rounded_weights, preferred_element_type=jnp.float32)
    partial_fresh = partial_fresh.astype(jnp.bfloat16).reshape(-1, 2, block_width // 2)
    fresh_terms = lax.all_to_all(partial_fresh, REP + TP, 0, 0, tiled=True)
    fresh_terms = fresh_terms.reshape(lax.axis_size(REP), lax.axis_size(TP), block_width)
    fresh_output = jnp.sum(fresh_terms.astype(jnp.float32), axis=1).astype(jnp.bfloat16)
    fresh_output = fresh_output.reshape(1, -1)
    attended = attend(queries, key_cache_slots, value_cache_slots, cache_lengths, fresh_output)
    return (master_new, first_new, second_new, attended)


def solution(mesh):
    fine = Mesh(mesh.devices.reshape(mesh.devices.shape[0], -1, 2, 2, 8), FINE_AXES)
    placed = (
        P("side", REP, TP),
        P("side", REP + TP, None),
        P(TP, REP),
        P(TP, REP),
        P(TP, REP),
        P(("side",) + REP, TP),
        P(("side",) + REP + TP, None),
        P(("side",) + REP + TP, None, None),
        P(("side",) + REP + TP, None, None),
        P(("side",) + REP + TP),
    )
    return jax.shard_map(
        local,
        mesh=fine,
        in_specs=placed,
        out_specs=(P(TP, REP), P(TP, REP), P(TP, REP), P(("side",) + REP + TP, None)),
        check_vma=False,
    )
```

```python
import functools

import jax
import jax.numpy as jnp
from jax import lax
from jax.experimental import pallas as pl
from jax.experimental.pallas import tpu as pltpu
from jax.sharding import Mesh
from jax.sharding import PartitionSpec as P

QUERY_HEADS = 64
KEY_VALUE_HEADS = 8
HEAD_SIZE = 128
STEP = 10


BETA_FIRST = 0.9
BETA_SECOND = 0.95
ADAM_EPSILON = 1e-08
LEARN_RATE = 0.001
DECAY_RATE = 0.1


def adamw(master, first_moment, second_moment, gradient):
    first_full = BETA_FIRST * first_moment.astype(jnp.float32) + (1.0 - BETA_FIRST) * gradient
    second_full = (
        BETA_SECOND * second_moment.astype(jnp.float32) + (1.0 - BETA_SECOND) * gradient * gradient
    )
    first_fix = 1.0 - BETA_FIRST**STEP
    second_fix = 1.0 - BETA_SECOND**STEP
    update = first_full / first_fix / (jnp.sqrt(second_full / second_fix) + ADAM_EPSILON)
    master_new = master - LEARN_RATE * (update + DECAY_RATE * master)
    return (master_new, first_full.astype(jnp.bfloat16), second_full.astype(jnp.bfloat16))


def attend(queries, key_cache_slots, value_cache_slots, cache_lengths, fresh_output):
    decode_row_count = queries.shape[0]
    slot_length = key_cache_slots.shape[1]
    query_groups = QUERY_HEADS // KEY_VALUE_HEADS
    query_head_rows = queries.reshape(decode_row_count, KEY_VALUE_HEADS, query_groups, HEAD_SIZE)
    stored_keys = key_cache_slots.reshape(decode_row_count, slot_length, KEY_VALUE_HEADS, HEAD_SIZE)
    stored_values = value_cache_slots.reshape(
        decode_row_count, slot_length, KEY_VALUE_HEADS, HEAD_SIZE
    )
    newest_keys = fresh_output[:, : KEY_VALUE_HEADS * HEAD_SIZE].reshape(
        decode_row_count, KEY_VALUE_HEADS, HEAD_SIZE
    )
    newest_values = fresh_output[:, KEY_VALUE_HEADS * HEAD_SIZE :].reshape(
        decode_row_count, KEY_VALUE_HEADS, HEAD_SIZE
    )
    score_scale = HEAD_SIZE ** (-0.5)
    scores = (
        jnp.einsum(
            "bkgd,blkd->bkgl", query_head_rows, stored_keys, preferred_element_type=jnp.float32
        )
        * score_scale
    )
    visible = jnp.arange(slot_length, dtype=jnp.int32)[None, :] < cache_lengths[:, None]
    scores = jnp.where(visible[:, None, None, :], scores, -1e30)
    self_score = (
        jnp.einsum(
            "zwai,zwi->zwa", query_head_rows, newest_keys, preferred_element_type=jnp.float32
        )
        * score_scale
    )
    highest = jnp.maximum(jnp.max(scores, axis=-1), self_score)
    weights = jnp.exp(scores - highest[..., None])
    own_weight = jnp.exp(self_score - highest)
    denominator = jnp.sum(weights, axis=-1) + own_weight
    probabilities = (weights / denominator[..., None]).astype(jnp.bfloat16)
    own_prob = (own_weight / denominator).astype(jnp.bfloat16)
    mixed = jnp.einsum(
        "bkgl,blkd->bkgd", probabilities, stored_values, preferred_element_type=jnp.float32
    )
    mixed = (
        mixed
        + own_prob.astype(jnp.float32)[..., None] * newest_values.astype(jnp.float32)[:, :, None, :]
    )
    return mixed.reshape(decode_row_count, QUERY_HEADS * HEAD_SIZE).astype(jnp.bfloat16)


FINE_AXES = ("side", "x", "core", "zhi", "y")
REP = ("x", "core")
TP = ("zhi", "y")


def swap_over(array, axis):
    return lax.ppermute(array, axis, [(0, 1), (1, 0)])


def shifted(array, axis, by):
    count = lax.axis_size(axis)
    return lax.ppermute(array, axis, [(i, (i + by) % count) for i in range(count)])


def from_behind(array, axis):
    return [array] + [shifted(array, axis, by) for by in range(1, lax.axis_size(axis))]


def product_kernel(for_other, position, *refs):
    *inputs, grads, out = refs
    half, along, core = position[0], position[1], position[2]
    y_count, x_count, rows, _ = grads.shape
    half_rows = y_count * rows
    feature_count = inputs[0].shape[1]
    width = out.shape[1]
    column = 1 - core if for_other else core
    columns = pl.ds(pl.multiple_of(column * width, width), width)
    sources = [lax.rem(along - behind + x_count, x_count) for behind in range(x_count)]
    right = jnp.concatenate(
        [grads[y, source, :, columns] for source in sources for y in range(y_count)]
    )
    for blocks, place in ((inputs[:x_count], half), (inputs[x_count:], 1 - half)):
        left = jnp.concatenate([block[:half_rows, :] for block in blocks])
        target = pl.ds(pl.multiple_of(place * feature_count, feature_count), feature_count)
        out[target, :] = lax.dot_general(
            left, right, (((0,), (0,)), ((), ())), preferred_element_type=jnp.float32
        ).astype(out.dtype)
    if for_other:
        decode_rows = inputs[0].shape[0] - half_rows
        for part in range(feature_count // width):
            for block, source in zip(inputs[:x_count], sources):
                start = 2 * feature_count + (part * x_count + source) * decode_rows
                target = pl.ds(pl.multiple_of(start, decode_rows), decode_rows)
                out[target, :] = block[half_rows:, part * width : (part + 1) * width]


def products(for_other, inputs, grads, width):
    feature_count = inputs[0].shape[1]
    position = jnp.stack([lax.axis_index(axis) for axis in ("zhi", "x", "core")]).astype(jnp.int32)
    y_count, x_count, rows, _ = grads.shape
    extra = 0
    if for_other:
        extra = (inputs[0].shape[0] - y_count * rows) * x_count * feature_count // width
    dtype = jnp.bfloat16 if for_other else jnp.float32
    return pl.pallas_call(
        functools.partial(product_kernel, for_other),
        out_shape=jax.ShapeDtypeStruct((2 * feature_count + extra, width), dtype),
        in_specs=[pl.BlockSpec(memory_space=pltpu.SMEM)]
        + [pl.BlockSpec(memory_space=pltpu.VMEM)] * (len(inputs) + 1),
        out_specs=pl.BlockSpec(memory_space=pltpu.VMEM),
        compiler_params=pltpu.CompilerParams(vmem_limit_bytes=32 * 2**20),
        cost_estimate=pl.CostEstimate(
            flops=4 * feature_count * y_count * x_count * rows * width,
            bytes_accessed=7 * 2**20,
            transcendentals=0,
        ),
        name="products_other" if for_other else "products_own",
    )(position, *inputs, grads)


def summed(terms):
    return jnp.sum(terms.astype(jnp.float32), axis=0).astype(jnp.bfloat16)


def local(
    learn_inputs,
    learn_grads,
    kv_master,
    first_moment,
    second_moment,
    decode_inputs,
    queries,
    key_cache_slots,
    value_cache_slots,
    cache_lengths,
):
    core, half = lax.axis_index("core"), lax.axis_index("zhi")
    x_count, side_count = lax.axis_size("x"), lax.axis_size("side")
    feature_count = learn_inputs.shape[2]
    block_width = kv_master.shape[1]
    quarter = feature_count // side_count

    row_halves = learn_inputs[0].reshape(2, -1, feature_count)
    received = swap_over(jnp.where(half == 0, row_halves[1], row_halves[0]), "zhi")
    kept = jnp.concatenate([jnp.where(half == 0, row_halves[0], row_halves[1]), decode_inputs])

    columns = learn_grads[0].reshape(-1, x_count, 2 * block_width).transpose(1, 0, 2)
    piece = lax.all_to_all(columns, "x", 0, 0, tiled=True)
    piece, kept = lax.optimization_barrier((piece, kept))
    grads_all = lax.all_gather(piece, "y", axis=0)
    inputs = from_behind(kept, "x") + from_behind(received, "x")

    sent = products(True, inputs, grads_all, block_width)
    sent_back = swap_over(sent, "core")
    kept_sum = products(False, inputs, grads_all, block_width)
    over_rep = (kept_sum + sent_back[: 2 * feature_count].astype(jnp.float32)).astype(jnp.bfloat16)
    over_x = over_rep.reshape(2 * side_count, quarter, block_width)
    decode_of_core = [
        jnp.concatenate(jnp.split(array[2 * feature_count :], feature_count // block_width), axis=1)
        for array in (sent, sent_back)
    ]
    decode_of_core = [array.reshape(x_count, -1, feature_count) for array in decode_of_core]
    decode_rows = jnp.where(
        core == 0, jnp.stack(decode_of_core, 1), jnp.stack(decode_of_core[::-1], 1)
    ).reshape(-1, feature_count)
    own_quarter = summed(lax.all_to_all(over_x, ("zhi", "side"), 0, 0, tiled=True))
    spread = jnp.broadcast_to(own_quarter[None], (side_count, quarter, block_width))
    gradient = lax.all_to_all(spread, "side", 0, 0, tiled=True)
    gradient = gradient.reshape(feature_count, block_width).astype(jnp.float32)
    master_new, first_new, second_new = adamw(kv_master, first_moment, second_moment, gradient)
    rounded_weights = master_new.astype(jnp.bfloat16)
    partial_fresh = jnp.dot(decode_rows, rounded_weights, preferred_element_type=jnp.float32)
    partial_fresh = partial_fresh.astype(jnp.bfloat16).reshape(-1, 2, block_width // 2)
    fresh_terms = lax.all_to_all(partial_fresh, REP + TP, 0, 0, tiled=True)
    fresh_terms = fresh_terms.reshape(lax.axis_size(REP), lax.axis_size(TP), block_width)
    fresh_output = jnp.sum(fresh_terms.astype(jnp.float32), axis=1).astype(jnp.bfloat16)
    fresh_output = fresh_output.reshape(1, -1)
    attended = attend(queries, key_cache_slots, value_cache_slots, cache_lengths, fresh_output)
    return (master_new, first_new, second_new, attended)


def solution(mesh):
    fine = Mesh(mesh.devices.reshape(mesh.devices.shape[0], -1, 2, 2, 8), FINE_AXES)
    placed = (
        P("side", REP, TP),
        P("side", REP + TP, None),
        P(TP, REP),
        P(TP, REP),
        P(TP, REP),
        P(("side",) + REP, TP),
        P(("side",) + REP + TP, None),
        P(("side",) + REP + TP, None, None),
        P(("side",) + REP + TP, None, None),
        P(("side",) + REP + TP),
    )
    return jax.shard_map(
        local,
        mesh=fine,
        in_specs=placed,
        out_specs=(P(TP, REP), P(TP, REP), P(TP, REP), P(("side",) + REP + TP, None)),
        check_vma=False,
    )
```

```python
import functools

import jax
import jax.numpy as jnp
from jax import lax
from jax.experimental import pallas as pl
from jax.experimental.pallas import tpu as pltpu
from jax.sharding import Mesh
from jax.sharding import PartitionSpec as P

QUERY_HEADS = 64
KEY_VALUE_HEADS = 8
HEAD_SIZE = 128
STEP = 10


BETA_FIRST = 0.9
BETA_SECOND = 0.95
ADAM_EPSILON = 1e-08
LEARN_RATE = 0.001
DECAY_RATE = 0.1


def adamw(master, first_moment, second_moment, gradient):
    first_full = BETA_FIRST * first_moment.astype(jnp.float32) + (1.0 - BETA_FIRST) * gradient
    second_full = (
        BETA_SECOND * second_moment.astype(jnp.float32) + (1.0 - BETA_SECOND) * gradient * gradient
    )
    first_fix = 1.0 - BETA_FIRST**STEP
    second_fix = 1.0 - BETA_SECOND**STEP
    update = first_full / first_fix / (jnp.sqrt(second_full / second_fix) + ADAM_EPSILON)
    master_new = master - LEARN_RATE * (update + DECAY_RATE * master)
    return (master_new, first_full.astype(jnp.bfloat16), second_full.astype(jnp.bfloat16))


def attend(queries, key_cache_slots, value_cache_slots, cache_lengths, fresh_output):
    decode_row_count = queries.shape[0]
    slot_length = key_cache_slots.shape[1]
    query_groups = QUERY_HEADS // KEY_VALUE_HEADS
    query_head_rows = queries.reshape(decode_row_count, KEY_VALUE_HEADS, query_groups, HEAD_SIZE)
    stored_keys = key_cache_slots.reshape(decode_row_count, slot_length, KEY_VALUE_HEADS, HEAD_SIZE)
    stored_values = value_cache_slots.reshape(
        decode_row_count, slot_length, KEY_VALUE_HEADS, HEAD_SIZE
    )
    newest_keys = fresh_output[:, : KEY_VALUE_HEADS * HEAD_SIZE].reshape(
        decode_row_count, KEY_VALUE_HEADS, HEAD_SIZE
    )
    newest_values = fresh_output[:, KEY_VALUE_HEADS * HEAD_SIZE :].reshape(
        decode_row_count, KEY_VALUE_HEADS, HEAD_SIZE
    )
    score_scale = HEAD_SIZE ** (-0.5)
    scores = (
        jnp.einsum(
            "bkgd,blkd->bkgl", query_head_rows, stored_keys, preferred_element_type=jnp.float32
        )
        * score_scale
    )
    visible = jnp.arange(slot_length, dtype=jnp.int32)[None, :] < cache_lengths[:, None]
    scores = jnp.where(visible[:, None, None, :], scores, -1e30)
    self_score = (
        jnp.einsum(
            "zwai,zwi->zwa", query_head_rows, newest_keys, preferred_element_type=jnp.float32
        )
        * score_scale
    )
    highest = jnp.maximum(jnp.max(scores, axis=-1), self_score)
    weights = jnp.exp(scores - highest[..., None])
    own_weight = jnp.exp(self_score - highest)
    denominator = jnp.sum(weights, axis=-1) + own_weight
    probabilities = (weights / denominator[..., None]).astype(jnp.bfloat16)
    own_prob = (own_weight / denominator).astype(jnp.bfloat16)
    mixed = jnp.einsum(
        "bkgl,blkd->bkgd", probabilities, stored_values, preferred_element_type=jnp.float32
    )
    mixed = (
        mixed
        + own_prob.astype(jnp.float32)[..., None] * newest_values.astype(jnp.float32)[:, :, None, :]
    )
    return mixed.reshape(decode_row_count, QUERY_HEADS * HEAD_SIZE).astype(jnp.bfloat16)


FINE_AXES = ("side", "x", "core", "zhi", "y")
REP = ("x", "core")
TP = ("zhi", "y")


def swap_over(array, axis):
    return lax.ppermute(array, axis, [(0, 1), (1, 0)])


def shifted(array, axis, by):
    count = lax.axis_size(axis)
    return lax.ppermute(array, axis, [(i, (i + by) % count) for i in range(count)])


def around_x(kept, received):
    half = received.shape[0] // 2
    upper, lower = [received[:half]], [received[half:]]
    for step in range(lax.axis_size("x") - 1):
        if step == 1:
            kept, *ends = lax.optimization_barrier((kept, upper[-1], lower[-1]))
            upper[-1], lower[-1] = ends
        upper.append(shifted(upper[-1], "x", 1))
        lower.append(shifted(lower[-1], "x", -1))
    behind, ahead = shifted(kept, "x", 1), shifted(kept, "x", -1)
    across = jnp.concatenate([shifted(behind[:half], "x", 1), shifted(ahead[half:], "x", -1)])
    parts = [part for pair in zip(upper[1:], lower[:0:-1]) for part in pair]
    return [kept, behind, across, ahead], [received, *parts]


def product_kernel(for_other, position, *refs):
    *inputs, grads, out = refs
    half, along, core = position[0], position[1], position[2]
    y_count, x_count, rows, _ = grads.shape
    half_rows = y_count * rows
    feature_count = inputs[0].shape[1]
    width = out.shape[1]
    column = 1 - core if for_other else core
    columns = pl.ds(pl.multiple_of(column * width, width), width)
    sources = [lax.rem(along - behind + x_count, x_count) for behind in range(x_count)]
    right = jnp.concatenate(
        [grads[y, source, :, columns] for source in sources for y in range(y_count)]
    )
    for blocks, place in ((inputs[:x_count], half), (inputs[x_count:], 1 - half)):
        left = jnp.concatenate([block[:half_rows, :] for block in blocks])
        target = pl.ds(pl.multiple_of(place * feature_count, feature_count), feature_count)
        out[target, :] = lax.dot_general(
            left, right, (((0,), (0,)), ((), ())), preferred_element_type=jnp.float32
        ).astype(out.dtype)
    if for_other:
        decode_rows = inputs[0].shape[0] - half_rows
        for part in range(feature_count // width):
            for block, source in zip(inputs[:x_count], sources):
                start = 2 * feature_count + (part * x_count + source) * decode_rows
                target = pl.ds(pl.multiple_of(start, decode_rows), decode_rows)
                out[target, :] = block[half_rows:, part * width : (part + 1) * width]


def products(for_other, inputs, grads, width):
    feature_count = inputs[0].shape[1]
    position = jnp.stack([lax.axis_index(axis) for axis in ("zhi", "x", "core")]).astype(jnp.int32)
    y_count, x_count, rows, _ = grads.shape
    extra = 0
    if for_other:
        extra = (inputs[0].shape[0] - y_count * rows) * x_count * feature_count // width
    dtype = jnp.bfloat16 if for_other else jnp.float32
    return pl.pallas_call(
        functools.partial(product_kernel, for_other),
        out_shape=jax.ShapeDtypeStruct((2 * feature_count + extra, width), dtype),
        in_specs=[pl.BlockSpec(memory_space=pltpu.SMEM)]
        + [pl.BlockSpec(memory_space=pltpu.VMEM)] * (len(inputs) + 1),
        out_specs=pl.BlockSpec(memory_space=pltpu.VMEM),
        compiler_params=pltpu.CompilerParams(vmem_limit_bytes=32 * 2**20),
        cost_estimate=pl.CostEstimate(
            flops=4 * feature_count * y_count * x_count * rows * width,
            bytes_accessed=7 * 2**20,
            transcendentals=0,
        ),
        name="products_other" if for_other else "products_own",
    )(position, *inputs, grads)


def summed(terms):
    return jnp.sum(terms.astype(jnp.float32), axis=0).astype(jnp.bfloat16)


def local(
    learn_inputs,
    learn_grads,
    kv_master,
    first_moment,
    second_moment,
    decode_inputs,
    queries,
    key_cache_slots,
    value_cache_slots,
    cache_lengths,
):
    core, half = lax.axis_index("core"), lax.axis_index("zhi")
    x_count, side_count = lax.axis_size("x"), lax.axis_size("side")
    feature_count = learn_inputs.shape[2]
    block_width = kv_master.shape[1]
    quarter = feature_count // side_count

    row_halves = learn_inputs[0].reshape(2, -1, feature_count)
    received = swap_over(jnp.where(half == 0, row_halves[1], row_halves[0]), "zhi")
    kept = jnp.concatenate([jnp.where(half == 0, row_halves[0], row_halves[1]), decode_inputs])

    columns = learn_grads[0].reshape(-1, x_count, 2 * block_width).transpose(1, 0, 2)
    piece = lax.all_to_all(columns, "x", 0, 0, tiled=True)
    piece, kept = lax.optimization_barrier((piece, kept))
    grads_all = lax.all_gather(piece, "y", axis=0)
    inputs = sum(around_x(kept, received), [])

    sent = products(True, inputs, grads_all, block_width)
    sent_back = swap_over(sent, "core")
    kept_sum = products(False, inputs, grads_all, block_width)
    over_rep = (kept_sum + sent_back[: 2 * feature_count].astype(jnp.float32)).astype(jnp.bfloat16)
    over_x = over_rep.reshape(2 * side_count, quarter, block_width)
    decode_of_core = [
        jnp.concatenate(jnp.split(array[2 * feature_count :], feature_count // block_width), axis=1)
        for array in (sent, sent_back)
    ]
    decode_of_core = [array.reshape(x_count, -1, feature_count) for array in decode_of_core]
    decode_rows = jnp.where(
        core == 0, jnp.stack(decode_of_core, 1), jnp.stack(decode_of_core[::-1], 1)
    ).reshape(-1, feature_count)
    own_quarter = summed(lax.all_to_all(over_x, ("zhi", "side"), 0, 0, tiled=True))
    spread = jnp.broadcast_to(own_quarter[None], (side_count, quarter, block_width))
    gradient = lax.all_to_all(spread, "side", 0, 0, tiled=True)
    gradient = gradient.reshape(feature_count, block_width).astype(jnp.float32)
    master_new, first_new, second_new = adamw(kv_master, first_moment, second_moment, gradient)
    rounded_weights = master_new.astype(jnp.bfloat16)
    partial_fresh = jnp.dot(decode_rows, rounded_weights, preferred_element_type=jnp.float32)
    partial_fresh = partial_fresh.astype(jnp.bfloat16).reshape(-1, 2, block_width // 2)
    fresh_terms = lax.all_to_all(partial_fresh, REP + TP, 0, 0, tiled=True)
    fresh_terms = fresh_terms.reshape(lax.axis_size(REP), lax.axis_size(TP), block_width)
    fresh_output = jnp.sum(fresh_terms.astype(jnp.float32), axis=1).astype(jnp.bfloat16)
    fresh_output = fresh_output.reshape(1, -1)
    attended = attend(queries, key_cache_slots, value_cache_slots, cache_lengths, fresh_output)
    return (master_new, first_new, second_new, attended)


def solution(mesh):
    fine = Mesh(mesh.devices.reshape(mesh.devices.shape[0], -1, 2, 2, 8), FINE_AXES)
    placed = (
        P("side", REP, TP),
        P("side", REP + TP, None),
        P(TP, REP),
        P(TP, REP),
        P(TP, REP),
        P(("side",) + REP, TP),
        P(("side",) + REP + TP, None),
        P(("side",) + REP + TP, None, None),
        P(("side",) + REP + TP, None, None),
        P(("side",) + REP + TP),
    )
    return jax.shard_map(
        local,
        mesh=fine,
        in_specs=placed,
        out_specs=(P(TP, REP), P(TP, REP), P(TP, REP), P(("side",) + REP + TP, None)),
        check_vma=False,
    )
```

```python
import functools

import jax
import jax.numpy as jnp
from jax import lax
from jax.experimental import pallas as pl
from jax.experimental.pallas import tpu as pltpu
from jax.sharding import Mesh
from jax.sharding import PartitionSpec as P

QUERY_HEADS = 64
KEY_VALUE_HEADS = 8
HEAD_SIZE = 128
STEP = 10


BETA_FIRST = 0.9
BETA_SECOND = 0.95
ADAM_EPSILON = 1e-08
LEARN_RATE = 0.001
DECAY_RATE = 0.1


def adamw(master, first_moment, second_moment, gradient):
    first_full = BETA_FIRST * first_moment.astype(jnp.float32) + (1.0 - BETA_FIRST) * gradient
    second_full = (
        BETA_SECOND * second_moment.astype(jnp.float32) + (1.0 - BETA_SECOND) * gradient * gradient
    )
    first_fix = 1.0 - BETA_FIRST**STEP
    second_fix = 1.0 - BETA_SECOND**STEP
    update = first_full / first_fix / (jnp.sqrt(second_full / second_fix) + ADAM_EPSILON)
    master_new = master - LEARN_RATE * (update + DECAY_RATE * master)
    return (master_new, first_full.astype(jnp.bfloat16), second_full.astype(jnp.bfloat16))


def attend(queries, key_cache_slots, value_cache_slots, cache_lengths, fresh_output):
    decode_row_count = queries.shape[0]
    slot_length = key_cache_slots.shape[1]
    query_groups = QUERY_HEADS // KEY_VALUE_HEADS
    query_head_rows = queries.reshape(decode_row_count, KEY_VALUE_HEADS, query_groups, HEAD_SIZE)
    stored_keys = key_cache_slots.reshape(decode_row_count, slot_length, KEY_VALUE_HEADS, HEAD_SIZE)
    stored_values = value_cache_slots.reshape(
        decode_row_count, slot_length, KEY_VALUE_HEADS, HEAD_SIZE
    )
    newest_keys = fresh_output[:, : KEY_VALUE_HEADS * HEAD_SIZE].reshape(
        decode_row_count, KEY_VALUE_HEADS, HEAD_SIZE
    )
    newest_values = fresh_output[:, KEY_VALUE_HEADS * HEAD_SIZE :].reshape(
        decode_row_count, KEY_VALUE_HEADS, HEAD_SIZE
    )
    score_scale = HEAD_SIZE ** (-0.5)
    scores = (
        jnp.einsum(
            "bkgd,blkd->bkgl", query_head_rows, stored_keys, preferred_element_type=jnp.float32
        )
        * score_scale
    )
    visible = jnp.arange(slot_length, dtype=jnp.int32)[None, :] < cache_lengths[:, None]
    scores = jnp.where(visible[:, None, None, :], scores, -1e30)
    self_score = (
        jnp.einsum(
            "zwai,zwi->zwa", query_head_rows, newest_keys, preferred_element_type=jnp.float32
        )
        * score_scale
    )
    highest = jnp.maximum(jnp.max(scores, axis=-1), self_score)
    weights = jnp.exp(scores - highest[..., None])
    own_weight = jnp.exp(self_score - highest)
    denominator = jnp.sum(weights, axis=-1) + own_weight
    probabilities = (weights / denominator[..., None]).astype(jnp.bfloat16)
    own_prob = (own_weight / denominator).astype(jnp.bfloat16)
    mixed = jnp.einsum(
        "bkgl,blkd->bkgd", probabilities, stored_values, preferred_element_type=jnp.float32
    )
    mixed = (
        mixed
        + own_prob.astype(jnp.float32)[..., None] * newest_values.astype(jnp.float32)[:, :, None, :]
    )
    return mixed.reshape(decode_row_count, QUERY_HEADS * HEAD_SIZE).astype(jnp.bfloat16)


FINE_AXES = ("side", "x", "core", "zhi", "y")
REP = ("x", "core")
TP = ("zhi", "y")


def swap_over(array, axis):
    return lax.ppermute(array, axis, [(0, 1), (1, 0)])


def shifted(array, axis, by):
    count = lax.axis_size(axis)
    return lax.ppermute(array, axis, [(i, (i + by) % count) for i in range(count)])


def from_behind(array, axis):
    return [array] + [shifted(array, axis, by) for by in range(1, lax.axis_size(axis))]


def same_kernel(array, out):
    pass


def held(array):
    return pl.pallas_call(
        same_kernel,
        out_shape=jax.ShapeDtypeStruct(array.shape, array.dtype),
        in_specs=[pl.BlockSpec(memory_space=pl.ANY)],
        out_specs=pl.BlockSpec(memory_space=pl.ANY),
        input_output_aliases={0: 0},
        cost_estimate=pl.CostEstimate(flops=50 * 10**9, bytes_accessed=0, transcendentals=0),
        name="held",
    )(array)


def product_kernel(for_other, position, *refs):
    *inputs, grads, out = refs
    half, along, core = position[0], position[1], position[2]
    y_count, x_count, rows, _ = grads.shape
    half_rows = y_count * rows
    feature_count = inputs[0].shape[1]
    width = out.shape[1]
    column = 1 - core if for_other else core
    columns = pl.ds(pl.multiple_of(column * width, width), width)
    sources = [lax.rem(along - behind + x_count, x_count) for behind in range(x_count)]
    right = jnp.concatenate(
        [grads[y, source, :, columns] for source in sources for y in range(y_count)]
    )
    for blocks, place in ((inputs[:x_count], half), (inputs[x_count:], 1 - half)):
        left = jnp.concatenate([block[:half_rows, :] for block in blocks])
        target = pl.ds(pl.multiple_of(place * feature_count, feature_count), feature_count)
        out[target, :] = lax.dot_general(
            left, right, (((0,), (0,)), ((), ())), preferred_element_type=jnp.float32
        ).astype(out.dtype)
    if for_other:
        decode_rows = inputs[0].shape[0] - half_rows
        for part in range(feature_count // width):
            for block, source in zip(inputs[:x_count], sources):
                start = 2 * feature_count + (part * x_count + source) * decode_rows
                target = pl.ds(pl.multiple_of(start, decode_rows), decode_rows)
                out[target, :] = block[half_rows:, part * width : (part + 1) * width]


def products(for_other, inputs, grads, width):
    feature_count = inputs[0].shape[1]
    position = jnp.stack([lax.axis_index(axis) for axis in ("zhi", "x", "core")]).astype(jnp.int32)
    y_count, x_count, rows, _ = grads.shape
    extra = 0
    if for_other:
        extra = (inputs[0].shape[0] - y_count * rows) * x_count * feature_count // width
    dtype = jnp.bfloat16 if for_other else jnp.float32
    return pl.pallas_call(
        functools.partial(product_kernel, for_other),
        out_shape=jax.ShapeDtypeStruct((2 * feature_count + extra, width), dtype),
        in_specs=[pl.BlockSpec(memory_space=pltpu.SMEM)]
        + [pl.BlockSpec(memory_space=pltpu.VMEM)] * (len(inputs) + 1),
        out_specs=pl.BlockSpec(memory_space=pltpu.VMEM),
        compiler_params=pltpu.CompilerParams(vmem_limit_bytes=32 * 2**20),
        cost_estimate=pl.CostEstimate(
            flops=4 * feature_count * y_count * x_count * rows * width,
            bytes_accessed=7 * 2**20,
            transcendentals=0,
        ),
        name="products_other" if for_other else "products_own",
    )(position, *inputs, grads)


def summed(terms):
    return jnp.sum(terms.astype(jnp.float32), axis=0).astype(jnp.bfloat16)


def local(
    learn_inputs,
    learn_grads,
    kv_master,
    first_moment,
    second_moment,
    decode_inputs,
    queries,
    key_cache_slots,
    value_cache_slots,
    cache_lengths,
):
    core, half = lax.axis_index("core"), lax.axis_index("zhi")
    x_count, side_count = lax.axis_size("x"), lax.axis_size("side")
    feature_count = learn_inputs.shape[2]
    block_width = kv_master.shape[1]
    quarter = feature_count // side_count

    row_halves = learn_inputs[0].reshape(2, -1, feature_count)
    received = swap_over(jnp.where(half == 0, row_halves[1], row_halves[0]), "zhi")
    kept = jnp.concatenate([jnp.where(half == 0, row_halves[0], row_halves[1]), decode_inputs])

    width = 2 * block_width
    columns = jnp.stack([learn_grads[0, :, i * width : (i + 1) * width] for i in range(x_count)])
    piece = lax.all_to_all(columns, "x", 0, 0, tiled=True)
    piece, kept = lax.optimization_barrier((piece, kept))
    y_count = lax.axis_size("y")
    grads_all = lax.all_to_all(jnp.broadcast_to(piece[None], (y_count, *piece.shape)), "y", 0, 0)
    behind = shifted(kept, "x", 1)
    kept, received = lax.optimization_barrier((kept, held(received)))
    inputs = [kept, behind, shifted(kept, "x", 2), shifted(kept, "x", 3)]
    inputs += from_behind(received, "x")

    sent = products(True, inputs, grads_all, block_width)
    sent_back = swap_over(sent, "core")
    kept_sum = products(False, inputs, grads_all, block_width)
    over_rep = (kept_sum + sent_back[: 2 * feature_count].astype(jnp.float32)).astype(jnp.bfloat16)
    over_x = over_rep.reshape(2 * side_count, quarter, block_width)
    decode_of_core = [
        jnp.concatenate(jnp.split(array[2 * feature_count :], feature_count // block_width), axis=1)
        for array in (sent, sent_back)
    ]
    decode_of_core = [array.reshape(x_count, -1, feature_count) for array in decode_of_core]
    decode_rows = jnp.where(
        core == 0, jnp.stack(decode_of_core, 1), jnp.stack(decode_of_core[::-1], 1)
    ).reshape(-1, feature_count)
    own_quarter = summed(lax.all_to_all(over_x, ("zhi", "side"), 0, 0, tiled=True))
    spread = jnp.broadcast_to(own_quarter[None], (side_count, quarter, block_width))
    gradient = lax.all_to_all(spread, "side", 0, 0, tiled=True)
    gradient = gradient.reshape(feature_count, block_width).astype(jnp.float32)
    master_new, first_new, second_new = adamw(kv_master, first_moment, second_moment, gradient)
    rounded_weights = master_new.astype(jnp.bfloat16)
    partial_fresh = jnp.dot(decode_rows, rounded_weights, preferred_element_type=jnp.float32)
    partial_fresh = partial_fresh.astype(jnp.bfloat16).reshape(-1, 2, block_width // 2)
    fresh_terms = lax.all_to_all(partial_fresh, REP + TP, 0, 0, tiled=True)
    fresh_terms = fresh_terms.reshape(lax.axis_size(REP), lax.axis_size(TP), block_width)
    fresh_output = jnp.sum(fresh_terms.astype(jnp.float32), axis=1).astype(jnp.bfloat16)
    fresh_output = fresh_output.reshape(1, -1)
    attended = attend(queries, key_cache_slots, value_cache_slots, cache_lengths, fresh_output)
    return (master_new, first_new, second_new, attended)


def solution(mesh):
    fine = Mesh(mesh.devices.reshape(mesh.devices.shape[0], -1, 2, 2, 8), FINE_AXES)
    placed = (
        P("side", REP, TP),
        P("side", REP + TP, None),
        P(TP, REP),
        P(TP, REP),
        P(TP, REP),
        P(("side",) + REP, TP),
        P(("side",) + REP + TP, None),
        P(("side",) + REP + TP, None, None),
        P(("side",) + REP + TP, None, None),
        P(("side",) + REP + TP),
    )
    return jax.shard_map(
        local,
        mesh=fine,
        in_specs=placed,
        out_specs=(P(TP, REP), P(TP, REP), P(TP, REP), P(("side",) + REP + TP, None)),
        check_vma=False,
    )
```

```python
import functools

import jax
import jax.numpy as jnp
from jax import lax
from jax.experimental import pallas as pl
from jax.experimental.pallas import tpu as pltpu
from jax.sharding import Mesh
from jax.sharding import PartitionSpec as P

QUERY_HEADS = 64
KEY_VALUE_HEADS = 8
HEAD_SIZE = 128
STEP = 10


BETA_FIRST = 0.9
BETA_SECOND = 0.95
ADAM_EPSILON = 1e-08
LEARN_RATE = 0.001
DECAY_RATE = 0.1


def adamw(master, first_moment, second_moment, gradient):
    first_full = BETA_FIRST * first_moment.astype(jnp.float32) + (1.0 - BETA_FIRST) * gradient
    second_full = (
        BETA_SECOND * second_moment.astype(jnp.float32) + (1.0 - BETA_SECOND) * gradient * gradient
    )
    first_fix = 1.0 - BETA_FIRST**STEP
    second_fix = 1.0 - BETA_SECOND**STEP
    update = first_full / first_fix / (jnp.sqrt(second_full / second_fix) + ADAM_EPSILON)
    master_new = master - LEARN_RATE * (update + DECAY_RATE * master)
    return (master_new, first_full.astype(jnp.bfloat16), second_full.astype(jnp.bfloat16))


def attend(queries, key_cache_slots, value_cache_slots, cache_lengths, fresh_output):
    decode_row_count = queries.shape[0]
    slot_length = key_cache_slots.shape[1]
    query_groups = QUERY_HEADS // KEY_VALUE_HEADS
    query_head_rows = queries.reshape(decode_row_count, KEY_VALUE_HEADS, query_groups, HEAD_SIZE)
    stored_keys = key_cache_slots.reshape(decode_row_count, slot_length, KEY_VALUE_HEADS, HEAD_SIZE)
    stored_values = value_cache_slots.reshape(
        decode_row_count, slot_length, KEY_VALUE_HEADS, HEAD_SIZE
    )
    newest_keys = fresh_output[:, : KEY_VALUE_HEADS * HEAD_SIZE].reshape(
        decode_row_count, KEY_VALUE_HEADS, HEAD_SIZE
    )
    newest_values = fresh_output[:, KEY_VALUE_HEADS * HEAD_SIZE :].reshape(
        decode_row_count, KEY_VALUE_HEADS, HEAD_SIZE
    )
    score_scale = HEAD_SIZE ** (-0.5)
    scores = (
        jnp.einsum(
            "bkgd,blkd->bkgl", query_head_rows, stored_keys, preferred_element_type=jnp.float32
        )
        * score_scale
    )
    visible = jnp.arange(slot_length, dtype=jnp.int32)[None, :] < cache_lengths[:, None]
    scores = jnp.where(visible[:, None, None, :], scores, -1e30)
    self_score = (
        jnp.einsum(
            "zwai,zwi->zwa", query_head_rows, newest_keys, preferred_element_type=jnp.float32
        )
        * score_scale
    )
    highest = jnp.maximum(jnp.max(scores, axis=-1), self_score)
    weights = jnp.exp(scores - highest[..., None])
    own_weight = jnp.exp(self_score - highest)
    denominator = jnp.sum(weights, axis=-1) + own_weight
    probabilities = (weights / denominator[..., None]).astype(jnp.bfloat16)
    own_prob = (own_weight / denominator).astype(jnp.bfloat16)
    mixed = jnp.einsum(
        "bkgl,blkd->bkgd", probabilities, stored_values, preferred_element_type=jnp.float32
    )
    mixed = (
        mixed
        + own_prob.astype(jnp.float32)[..., None] * newest_values.astype(jnp.float32)[:, :, None, :]
    )
    return mixed.reshape(decode_row_count, QUERY_HEADS * HEAD_SIZE).astype(jnp.bfloat16)


FINE_AXES = ("side", "x", "core", "zhi", "y")
REP = ("x", "core")
TP = ("zhi", "y")


def swap_over(array, axis):
    return lax.ppermute(array, axis, [(0, 1), (1, 0)])


def shifted(array, axis, by):
    count = lax.axis_size(axis)
    return lax.ppermute(array, axis, [(i, (i + by) % count) for i in range(count)])


def around(array, axis):
    half = array.shape[0] // 32 * 16
    behind, ahead = shifted(array, axis, 1), shifted(array, axis, -1)
    return [array, behind, shifted(behind[:half], axis, 1), shifted(ahead[half:], axis, -1), ahead]


def product_kernel(for_other, position, *refs):
    *inputs, grads, out = refs
    half, along, core = position[0], position[1], position[2]
    y_count, x_count, rows, _ = grads.shape
    half_rows = y_count * rows
    feature_count = inputs[0].shape[1]
    width = out.shape[1]
    column = 1 - core if for_other else core
    columns = pl.ds(pl.multiple_of(column * width, width), width)
    sources = [lax.rem(along - behind + x_count, x_count) for behind in range(x_count)]
    right = jnp.concatenate(
        [grads[y, source, :, columns] for source in sources for y in range(y_count)]
    )
    unit = half_rows // 2
    parts = len(inputs) // 2
    for blocks, place in ((inputs[:parts], half), (inputs[parts:], 1 - half)):
        left = jnp.concatenate([block[: block.shape[0] // unit * unit, :] for block in blocks])
        target = pl.ds(pl.multiple_of(place * feature_count, feature_count), feature_count)
        out[target, :] = lax.dot_general(
            left, right, (((0,), (0,)), ((), ())), preferred_element_type=jnp.float32
        ).astype(out.dtype)
    if for_other:
        decode_rows = inputs[0].shape[0] - half_rows
        below = [block for block in inputs[:parts] if block.shape[0] % unit]
        for part in range(feature_count // width):
            for block, source in zip(below, sources):
                start = 2 * feature_count + (part * x_count + source) * decode_rows
                target = pl.ds(pl.multiple_of(start, decode_rows), decode_rows)
                out[target, :] = block[
                    block.shape[0] - decode_rows :, part * width : (part + 1) * width
                ]


def products(for_other, inputs, grads, width):
    feature_count = inputs[0].shape[1]
    position = jnp.stack([lax.axis_index(axis) for axis in ("zhi", "x", "core")]).astype(jnp.int32)
    y_count, x_count, rows, _ = grads.shape
    extra = 0
    if for_other:
        extra = (inputs[0].shape[0] - y_count * rows) * x_count * feature_count // width
    dtype = jnp.bfloat16 if for_other else jnp.float32
    return pl.pallas_call(
        functools.partial(product_kernel, for_other),
        out_shape=jax.ShapeDtypeStruct((2 * feature_count + extra, width), dtype),
        in_specs=[pl.BlockSpec(memory_space=pltpu.SMEM)]
        + [pl.BlockSpec(memory_space=pltpu.VMEM)] * (len(inputs) + 1),
        out_specs=pl.BlockSpec(memory_space=pltpu.VMEM),
        compiler_params=pltpu.CompilerParams(vmem_limit_bytes=32 * 2**20),
        cost_estimate=pl.CostEstimate(
            flops=4 * feature_count * y_count * x_count * rows * width,
            bytes_accessed=7 * 2**20,
            transcendentals=0,
        ),
        name="products_other" if for_other else "products_own",
    )(position, *inputs, grads)


def summed(terms):
    return jnp.sum(terms.astype(jnp.float32), axis=0).astype(jnp.bfloat16)


def local(
    learn_inputs,
    learn_grads,
    kv_master,
    first_moment,
    second_moment,
    decode_inputs,
    queries,
    key_cache_slots,
    value_cache_slots,
    cache_lengths,
):
    core, half = lax.axis_index("core"), lax.axis_index("zhi")
    x_count, side_count = lax.axis_size("x"), lax.axis_size("side")
    feature_count = learn_inputs.shape[2]
    block_width = kv_master.shape[1]
    quarter = feature_count // side_count

    row_halves = learn_inputs[0].reshape(2, -1, feature_count)
    received = swap_over(jnp.where(half == 0, row_halves[1], row_halves[0]), "zhi")
    kept = jnp.concatenate([jnp.where(half == 0, row_halves[0], row_halves[1]), decode_inputs])

    width = 2 * block_width
    columns = jnp.stack([learn_grads[0, :, i * width : (i + 1) * width] for i in range(x_count)])
    piece = lax.all_to_all(columns, "x", 0, 0, tiled=True)
    piece, kept = lax.optimization_barrier((piece, kept))
    y_count = lax.axis_size("y")
    grads_all = lax.all_to_all(jnp.broadcast_to(piece[None], (y_count, *piece.shape)), "y", 0, 0)
    inputs = around(kept, "x") + around(received, "x")

    sent = products(True, inputs, grads_all, block_width)
    sent_back = swap_over(sent, "core")
    kept_sum = products(False, inputs, grads_all, block_width)
    over_rep = (kept_sum + sent_back[: 2 * feature_count].astype(jnp.float32)).astype(jnp.bfloat16)
    over_x = over_rep.reshape(2 * side_count, quarter, block_width)
    decode_of_core = [
        jnp.concatenate(jnp.split(array[2 * feature_count :], feature_count // block_width), axis=1)
        for array in (sent, sent_back)
    ]
    decode_of_core = [array.reshape(x_count, -1, feature_count) for array in decode_of_core]
    decode_rows = jnp.where(
        core == 0, jnp.stack(decode_of_core, 1), jnp.stack(decode_of_core[::-1], 1)
    ).reshape(-1, feature_count)
    own_quarter = summed(lax.all_to_all(over_x, ("zhi", "side"), 0, 0, tiled=True))
    spread = jnp.broadcast_to(own_quarter[None], (side_count, quarter, block_width))
    gradient = lax.all_to_all(spread, "side", 0, 0, tiled=True)
    gradient = gradient.reshape(feature_count, block_width).astype(jnp.float32)
    master_new, first_new, second_new = adamw(kv_master, first_moment, second_moment, gradient)
    rounded_weights = master_new.astype(jnp.bfloat16)
    partial_fresh = jnp.dot(decode_rows, rounded_weights, preferred_element_type=jnp.float32)
    partial_fresh = partial_fresh.astype(jnp.bfloat16).reshape(-1, 2, block_width // 2)
    fresh_terms = lax.all_to_all(partial_fresh, REP + TP, 0, 0, tiled=True)
    fresh_terms = fresh_terms.reshape(lax.axis_size(REP), lax.axis_size(TP), block_width)
    fresh_output = jnp.sum(fresh_terms.astype(jnp.float32), axis=1).astype(jnp.bfloat16)
    fresh_output = fresh_output.reshape(1, -1)
    attended = attend(queries, key_cache_slots, value_cache_slots, cache_lengths, fresh_output)
    return (master_new, first_new, second_new, attended)


def solution(mesh):
    fine = Mesh(mesh.devices.reshape(mesh.devices.shape[0], -1, 2, 2, 8), FINE_AXES)
    placed = (
        P("side", REP, TP),
        P("side", REP + TP, None),
        P(TP, REP),
        P(TP, REP),
        P(TP, REP),
        P(("side",) + REP, TP),
        P(("side",) + REP + TP, None),
        P(("side",) + REP + TP, None, None),
        P(("side",) + REP + TP, None, None),
        P(("side",) + REP + TP),
    )
    return jax.shard_map(
        local,
        mesh=fine,
        in_specs=placed,
        out_specs=(P(TP, REP), P(TP, REP), P(TP, REP), P(("side",) + REP + TP, None)),
        check_vma=False,
    )
```

```python
import functools

import jax
import jax.numpy as jnp
from jax import lax
from jax.experimental import pallas as pl
from jax.experimental.pallas import tpu as pltpu
from jax.sharding import Mesh
from jax.sharding import PartitionSpec as P

QUERY_HEADS = 64
KEY_VALUE_HEADS = 8
HEAD_SIZE = 128
STEP = 10


BETA_FIRST = 0.9
BETA_SECOND = 0.95
ADAM_EPSILON = 1e-08
LEARN_RATE = 0.001
DECAY_RATE = 0.1


def adamw(master, first_moment, second_moment, gradient):
    first_full = BETA_FIRST * first_moment.astype(jnp.float32) + (1.0 - BETA_FIRST) * gradient
    second_full = (
        BETA_SECOND * second_moment.astype(jnp.float32) + (1.0 - BETA_SECOND) * gradient * gradient
    )
    first_fix = 1.0 - BETA_FIRST**STEP
    second_fix = 1.0 - BETA_SECOND**STEP
    update = first_full / first_fix / (jnp.sqrt(second_full / second_fix) + ADAM_EPSILON)
    master_new = master - LEARN_RATE * (update + DECAY_RATE * master)
    return (master_new, first_full.astype(jnp.bfloat16), second_full.astype(jnp.bfloat16))


def attend(queries, key_cache_slots, value_cache_slots, cache_lengths, fresh_output):
    decode_row_count = queries.shape[0]
    slot_length = key_cache_slots.shape[1]
    query_groups = QUERY_HEADS // KEY_VALUE_HEADS
    query_head_rows = queries.reshape(decode_row_count, KEY_VALUE_HEADS, query_groups, HEAD_SIZE)
    stored_keys = key_cache_slots.reshape(decode_row_count, slot_length, KEY_VALUE_HEADS, HEAD_SIZE)
    stored_values = value_cache_slots.reshape(
        decode_row_count, slot_length, KEY_VALUE_HEADS, HEAD_SIZE
    )
    newest_keys = fresh_output[:, : KEY_VALUE_HEADS * HEAD_SIZE].reshape(
        decode_row_count, KEY_VALUE_HEADS, HEAD_SIZE
    )
    newest_values = fresh_output[:, KEY_VALUE_HEADS * HEAD_SIZE :].reshape(
        decode_row_count, KEY_VALUE_HEADS, HEAD_SIZE
    )
    score_scale = HEAD_SIZE ** (-0.5)
    scores = (
        jnp.einsum(
            "bkgd,blkd->bkgl", query_head_rows, stored_keys, preferred_element_type=jnp.float32
        )
        * score_scale
    )
    visible = jnp.arange(slot_length, dtype=jnp.int32)[None, :] < cache_lengths[:, None]
    scores = jnp.where(visible[:, None, None, :], scores, -1e30)
    self_score = (
        jnp.einsum(
            "zwai,zwi->zwa", query_head_rows, newest_keys, preferred_element_type=jnp.float32
        )
        * score_scale
    )
    highest = jnp.maximum(jnp.max(scores, axis=-1), self_score)
    weights = jnp.exp(scores - highest[..., None])
    own_weight = jnp.exp(self_score - highest)
    denominator = jnp.sum(weights, axis=-1) + own_weight
    probabilities = (weights / denominator[..., None]).astype(jnp.bfloat16)
    own_prob = (own_weight / denominator).astype(jnp.bfloat16)
    mixed = jnp.einsum(
        "bkgl,blkd->bkgd", probabilities, stored_values, preferred_element_type=jnp.float32
    )
    mixed = (
        mixed
        + own_prob.astype(jnp.float32)[..., None] * newest_values.astype(jnp.float32)[:, :, None, :]
    )
    return mixed.reshape(decode_row_count, QUERY_HEADS * HEAD_SIZE).astype(jnp.bfloat16)


FINE_AXES = ("side", "x", "core", "zhi", "y")
REP = ("x", "core")
TP = ("zhi", "y")


def swap_over(array, axis):
    return lax.ppermute(array, axis, [(0, 1), (1, 0)])


def shifted(array, axis, by):
    count = lax.axis_size(axis)
    return lax.ppermute(array, axis, [(i, (i + by) % count) for i in range(count)])


def around(array, axis, way):
    behind, ahead = shifted(array, axis, 1), shifted(array, axis, -1)
    across = shifted(behind if way == 1 else ahead, axis, way)
    return [array, behind, across, ahead]


def same_kernel(array, out):
    pass


def held(array):
    return pl.pallas_call(
        same_kernel,
        out_shape=jax.ShapeDtypeStruct(array.shape, array.dtype),
        in_specs=[pl.BlockSpec(memory_space=pl.ANY)],
        out_specs=pl.BlockSpec(memory_space=pl.ANY),
        input_output_aliases={0: 0},
        cost_estimate=pl.CostEstimate(flops=24 * 10**9, bytes_accessed=0, transcendentals=0),
        name="held",
    )(array)


def product_kernel(for_other, position, *refs):
    *inputs, grads, out = refs
    half, along, core = position[0], position[1], position[2]
    y_count, x_count, rows, _ = grads.shape
    half_rows = y_count * rows
    feature_count = inputs[0].shape[1]
    width = out.shape[1]
    column = 1 - core if for_other else core
    columns = pl.ds(pl.multiple_of(column * width, width), width)
    sources = [lax.rem(along - behind + x_count, x_count) for behind in range(x_count)]
    right = jnp.concatenate(
        [grads[y, source, :, columns] for source in sources for y in range(y_count)]
    )
    for blocks, place in ((inputs[:x_count], half), (inputs[x_count:], 1 - half)):
        left = jnp.concatenate([block[:half_rows, :] for block in blocks])
        target = pl.ds(pl.multiple_of(place * feature_count, feature_count), feature_count)
        out[target, :] = lax.dot_general(
            left, right, (((0,), (0,)), ((), ())), preferred_element_type=jnp.float32
        ).astype(out.dtype)
    if for_other:
        decode_rows = inputs[0].shape[0] - half_rows
        for part in range(feature_count // width):
            for block, source in zip(inputs[:x_count], sources):
                start = 2 * feature_count + (part * x_count + source) * decode_rows
                target = pl.ds(pl.multiple_of(start, decode_rows), decode_rows)
                out[target, :] = block[half_rows:, part * width : (part + 1) * width]


def products(for_other, inputs, grads, width):
    feature_count = inputs[0].shape[1]
    position = jnp.stack([lax.axis_index(axis) for axis in ("zhi", "x", "core")]).astype(jnp.int32)
    y_count, x_count, rows, _ = grads.shape
    extra = 0
    if for_other:
        extra = (inputs[0].shape[0] - y_count * rows) * x_count * feature_count // width
    dtype = jnp.bfloat16 if for_other else jnp.float32
    return pl.pallas_call(
        functools.partial(product_kernel, for_other),
        out_shape=jax.ShapeDtypeStruct((2 * feature_count + extra, width), dtype),
        in_specs=[pl.BlockSpec(memory_space=pltpu.SMEM)]
        + [pl.BlockSpec(memory_space=pltpu.VMEM)] * (len(inputs) + 1),
        out_specs=pl.BlockSpec(memory_space=pltpu.VMEM),
        compiler_params=pltpu.CompilerParams(vmem_limit_bytes=32 * 2**20),
        cost_estimate=pl.CostEstimate(
            flops=4 * feature_count * y_count * x_count * rows * width,
            bytes_accessed=7 * 2**20,
            transcendentals=0,
        ),
        name="products_other" if for_other else "products_own",
    )(position, *inputs, grads)


def summed(terms):
    return jnp.sum(terms.astype(jnp.float32), axis=0).astype(jnp.bfloat16)


def local(
    learn_inputs,
    learn_grads,
    kv_master,
    first_moment,
    second_moment,
    decode_inputs,
    queries,
    key_cache_slots,
    value_cache_slots,
    cache_lengths,
):
    core, half = lax.axis_index("core"), lax.axis_index("zhi")
    x_count, side_count = lax.axis_size("x"), lax.axis_size("side")
    feature_count = learn_inputs.shape[2]
    block_width = kv_master.shape[1]
    quarter = feature_count // side_count

    row_halves = learn_inputs[0].reshape(2, -1, feature_count)
    received = swap_over(jnp.where(half == 0, row_halves[1], row_halves[0]), "zhi")
    kept = jnp.concatenate([jnp.where(half == 0, row_halves[0], row_halves[1]), decode_inputs])

    width = 2 * block_width
    columns = jnp.stack([learn_grads[0, :, i * width : (i + 1) * width] for i in range(x_count)])
    piece = lax.all_to_all(columns, "x", 0, 0, tiled=True)
    piece, kept = lax.optimization_barrier((piece, kept))
    y_count = lax.axis_size("y")
    grads_all = lax.all_to_all(jnp.broadcast_to(piece[None], (y_count, *piece.shape)), "y", 0, 0)
    inputs = around(kept, "x", 1) + around(held(received), "x", -1)

    sent = products(True, inputs, grads_all, block_width)
    sent_back = swap_over(sent, "core")
    kept_sum = products(False, inputs, grads_all, block_width)
    over_rep = (kept_sum + sent_back[: 2 * feature_count].astype(jnp.float32)).astype(jnp.bfloat16)
    over_x = over_rep.reshape(2 * side_count, quarter, block_width)
    decode_of_core = [
        jnp.concatenate(jnp.split(array[2 * feature_count :], feature_count // block_width), axis=1)
        for array in (sent, sent_back)
    ]
    decode_of_core = [array.reshape(x_count, -1, feature_count) for array in decode_of_core]
    decode_rows = jnp.where(
        core == 0, jnp.stack(decode_of_core, 1), jnp.stack(decode_of_core[::-1], 1)
    ).reshape(-1, feature_count)
    own_quarter = summed(lax.all_to_all(over_x, ("zhi", "side"), 0, 0, tiled=True))
    spread = jnp.broadcast_to(own_quarter[None], (side_count, quarter, block_width))
    gradient = lax.all_to_all(spread, "side", 0, 0, tiled=True)
    gradient = gradient.reshape(feature_count, block_width).astype(jnp.float32)
    master_new, first_new, second_new = adamw(kv_master, first_moment, second_moment, gradient)
    rounded_weights = master_new.astype(jnp.bfloat16)
    partial_fresh = jnp.dot(decode_rows, rounded_weights, preferred_element_type=jnp.float32)
    partial_fresh = partial_fresh.astype(jnp.bfloat16).reshape(-1, 2, block_width // 2)
    fresh_terms = lax.all_to_all(partial_fresh, REP + TP, 0, 0, tiled=True)
    fresh_terms = fresh_terms.reshape(lax.axis_size(REP), lax.axis_size(TP), block_width)
    fresh_output = jnp.sum(fresh_terms.astype(jnp.float32), axis=1).astype(jnp.bfloat16)
    fresh_output = fresh_output.reshape(1, -1)
    attended = attend(queries, key_cache_slots, value_cache_slots, cache_lengths, fresh_output)
    return (master_new, first_new, second_new, attended)


def solution(mesh):
    fine = Mesh(mesh.devices.reshape(mesh.devices.shape[0], -1, 2, 2, 8), FINE_AXES)
    placed = (
        P("side", REP, TP),
        P("side", REP + TP, None),
        P(TP, REP),
        P(TP, REP),
        P(TP, REP),
        P(("side",) + REP, TP),
        P(("side",) + REP + TP, None),
        P(("side",) + REP + TP, None, None),
        P(("side",) + REP + TP, None, None),
        P(("side",) + REP + TP),
    )
    return jax.shard_map(
        local,
        mesh=fine,
        in_specs=placed,
        out_specs=(P(TP, REP), P(TP, REP), P(TP, REP), P(("side",) + REP + TP, None)),
        check_vma=False,
    )
```

```python
import functools

import jax
import jax.numpy as jnp
from jax import lax
from jax.experimental import pallas as pl
from jax.experimental.pallas import tpu as pltpu
from jax.sharding import Mesh
from jax.sharding import PartitionSpec as P

QUERY_HEADS = 64
KEY_VALUE_HEADS = 8
HEAD_SIZE = 128
STEP = 10


BETA_FIRST = 0.9
BETA_SECOND = 0.95
ADAM_EPSILON = 1e-08
LEARN_RATE = 0.001
DECAY_RATE = 0.1


def adamw(master, first_moment, second_moment, gradient):
    first_full = BETA_FIRST * first_moment.astype(jnp.float32) + (1.0 - BETA_FIRST) * gradient
    second_full = (
        BETA_SECOND * second_moment.astype(jnp.float32) + (1.0 - BETA_SECOND) * gradient * gradient
    )
    first_fix = 1.0 - BETA_FIRST**STEP
    second_fix = 1.0 - BETA_SECOND**STEP
    update = first_full / first_fix / (jnp.sqrt(second_full / second_fix) + ADAM_EPSILON)
    master_new = master - LEARN_RATE * (update + DECAY_RATE * master)
    return (master_new, first_full.astype(jnp.bfloat16), second_full.astype(jnp.bfloat16))


def attend(queries, key_cache_slots, value_cache_slots, cache_lengths, fresh_output):
    decode_row_count = queries.shape[0]
    slot_length = key_cache_slots.shape[1]
    query_groups = QUERY_HEADS // KEY_VALUE_HEADS
    query_head_rows = queries.reshape(decode_row_count, KEY_VALUE_HEADS, query_groups, HEAD_SIZE)
    stored_keys = key_cache_slots.reshape(decode_row_count, slot_length, KEY_VALUE_HEADS, HEAD_SIZE)
    stored_values = value_cache_slots.reshape(
        decode_row_count, slot_length, KEY_VALUE_HEADS, HEAD_SIZE
    )
    newest_keys = fresh_output[:, : KEY_VALUE_HEADS * HEAD_SIZE].reshape(
        decode_row_count, KEY_VALUE_HEADS, HEAD_SIZE
    )
    newest_values = fresh_output[:, KEY_VALUE_HEADS * HEAD_SIZE :].reshape(
        decode_row_count, KEY_VALUE_HEADS, HEAD_SIZE
    )
    score_scale = HEAD_SIZE ** (-0.5)
    scores = (
        jnp.einsum(
            "bkgd,blkd->bkgl", query_head_rows, stored_keys, preferred_element_type=jnp.float32
        )
        * score_scale
    )
    visible = jnp.arange(slot_length, dtype=jnp.int32)[None, :] < cache_lengths[:, None]
    scores = jnp.where(visible[:, None, None, :], scores, -1e30)
    self_score = (
        jnp.einsum(
            "zwai,zwi->zwa", query_head_rows, newest_keys, preferred_element_type=jnp.float32
        )
        * score_scale
    )
    highest = jnp.maximum(jnp.max(scores, axis=-1), self_score)
    weights = jnp.exp(scores - highest[..., None])
    own_weight = jnp.exp(self_score - highest)
    denominator = jnp.sum(weights, axis=-1) + own_weight
    probabilities = (weights / denominator[..., None]).astype(jnp.bfloat16)
    own_prob = (own_weight / denominator).astype(jnp.bfloat16)
    mixed = jnp.einsum(
        "bkgl,blkd->bkgd", probabilities, stored_values, preferred_element_type=jnp.float32
    )
    mixed = (
        mixed
        + own_prob.astype(jnp.float32)[..., None] * newest_values.astype(jnp.float32)[:, :, None, :]
    )
    return mixed.reshape(decode_row_count, QUERY_HEADS * HEAD_SIZE).astype(jnp.bfloat16)


FINE_AXES = ("side", "x", "core", "zhi", "y")
REP = ("x", "core")
TP = ("zhi", "y")


def swap_over(array, axis):
    return lax.ppermute(array, axis, [(0, 1), (1, 0)])


def shifted(array, axis, by):
    count = lax.axis_size(axis)
    return lax.ppermute(array, axis, [(i, (i + by) % count) for i in range(count)])


def around(array, axis, way):
    behind, ahead = shifted(array, axis, 1), shifted(array, axis, -1)
    across = shifted(behind if way == 1 else ahead, axis, way)
    return [array, behind, across, ahead]


def same_kernel(array, out):
    pass


def held(array):
    return pl.pallas_call(
        same_kernel,
        out_shape=jax.ShapeDtypeStruct(array.shape, array.dtype),
        in_specs=[pl.BlockSpec(memory_space=pl.ANY)],
        out_specs=pl.BlockSpec(memory_space=pl.ANY),
        input_output_aliases={0: 0},
        cost_estimate=pl.CostEstimate(flops=24 * 10**9, bytes_accessed=0, transcendentals=0),
        name="held",
    )(array)


def product_kernel(for_other, position, *refs):
    *inputs, grads, out = refs
    half, along, core = position[0], position[1], position[2]
    y_count, x_count, rows, _ = grads.shape
    half_rows = y_count * rows
    feature_count = inputs[0].shape[1]
    _, width, lanes = out.shape
    parts = feature_count // lanes
    column = 1 - core if for_other else core
    columns = pl.ds(pl.multiple_of(column * width, width), width)
    sources = [lax.rem(along - behind + x_count, x_count) for behind in range(x_count)]
    grads_rows = jnp.concatenate(
        [grads[y, source, :, columns] for source in sources for y in range(y_count)]
    )
    for blocks, place in ((inputs[:x_count], half), (inputs[x_count:], 1 - half)):
        inputs_rows = jnp.concatenate([block[:half_rows, :] for block in blocks])
        product = lax.dot_general(
            grads_rows,
            inputs_rows,
            (((0,), (0,)), ((), ())),
            preferred_element_type=jnp.float32,
        ).astype(out.dtype)
        for part in range(parts):
            out[place * parts + part] = product[:, part * lanes : (part + 1) * lanes]
    if for_other:
        decode_rows = inputs[0].shape[0] - half_rows
        for part in range(parts):
            for block, source in zip(inputs[:x_count], sources):
                start = (part * x_count + source) * decode_rows
                target = pl.ds(pl.multiple_of(start, decode_rows), decode_rows)
                out[2 * parts, target, :] = block[half_rows:, part * lanes : (part + 1) * lanes]


def products(for_other, inputs, grads, width, lanes):
    feature_count = inputs[0].shape[1]
    position = jnp.stack([lax.axis_index(axis) for axis in ("zhi", "x", "core")]).astype(jnp.int32)
    y_count, x_count, rows, _ = grads.shape
    blocks = 2 * feature_count // lanes + for_other
    dtype = jnp.bfloat16 if for_other else jnp.float32
    return pl.pallas_call(
        functools.partial(product_kernel, for_other),
        out_shape=jax.ShapeDtypeStruct((blocks, width, lanes), dtype),
        in_specs=[pl.BlockSpec(memory_space=pltpu.SMEM)]
        + [pl.BlockSpec(memory_space=pltpu.VMEM)] * (len(inputs) + 1),
        out_specs=pl.BlockSpec(memory_space=pltpu.VMEM),
        compiler_params=pltpu.CompilerParams(vmem_limit_bytes=32 * 2**20),
        cost_estimate=pl.CostEstimate(
            flops=4 * feature_count * y_count * x_count * rows * width,
            bytes_accessed=7 * 2**20,
            transcendentals=0,
        ),
        name="products_other" if for_other else "products_own",
    )(position, *inputs, grads)


def summed(terms):
    return jnp.sum(terms.astype(jnp.float32), axis=0).astype(jnp.bfloat16)


def local(
    learn_inputs,
    learn_grads,
    kv_master,
    first_moment,
    second_moment,
    decode_inputs,
    queries,
    key_cache_slots,
    value_cache_slots,
    cache_lengths,
):
    core, half = lax.axis_index("core"), lax.axis_index("zhi")
    x_count, side_count = lax.axis_size("x"), lax.axis_size("side")
    feature_count = learn_inputs.shape[2]
    block_width = kv_master.shape[1]
    quarter = feature_count // side_count

    row_halves = learn_inputs[0].reshape(2, -1, feature_count)
    received = swap_over(jnp.where(half == 0, row_halves[1], row_halves[0]), "zhi")
    kept = jnp.concatenate([jnp.where(half == 0, row_halves[0], row_halves[1]), decode_inputs])

    width = 2 * block_width
    columns = jnp.stack([learn_grads[0, :, i * width : (i + 1) * width] for i in range(x_count)])
    piece = lax.all_to_all(columns, "x", 0, 0, tiled=True)
    piece, kept = lax.optimization_barrier((piece, kept))
    y_count = lax.axis_size("y")
    grads_all = lax.all_to_all(jnp.broadcast_to(piece[None], (y_count, *piece.shape)), "y", 0, 0)
    behind, ahead = shifted(kept, "x", 1), shifted(kept, "x", -1)
    received = held(received)
    ahead, received = lax.optimization_barrier((ahead, received))
    inputs = [kept, behind, shifted(behind, "x", 1), ahead] + around(received, "x", -1)

    sent = products(True, inputs, grads_all, block_width, quarter)
    sent_back = swap_over(sent, "core")
    kept_sum = products(False, inputs, grads_all, block_width, quarter)
    over_rep = (kept_sum + sent_back[:-1].astype(jnp.float32)).astype(jnp.bfloat16)
    decode_of_core = [
        jnp.concatenate(jnp.split(array[-1], side_count), axis=1).reshape(x_count, -1, feature_count)
        for array in (sent, sent_back)
    ]
    decode_rows = jnp.where(
        core == 0, jnp.stack(decode_of_core, 1), jnp.stack(decode_of_core[::-1], 1)
    ).reshape(-1, feature_count)
    own_quarter = summed(lax.all_to_all(over_rep, ("zhi", "side"), 0, 0, tiled=True))
    spread = jnp.broadcast_to(own_quarter[None], (side_count, *own_quarter.shape))
    gradient = lax.all_to_all(spread, "side", 0, 0, tiled=True)
    gradient = gradient.transpose(0, 2, 1).reshape(feature_count, block_width).astype(jnp.float32)
    master_new, first_new, second_new = adamw(kv_master, first_moment, second_moment, gradient)
    rounded_weights = master_new.astype(jnp.bfloat16)
    partial_fresh = jnp.dot(decode_rows, rounded_weights, preferred_element_type=jnp.float32)
    partial_fresh = partial_fresh.astype(jnp.bfloat16).reshape(-1, 2, block_width // 2)
    fresh_terms = lax.all_to_all(partial_fresh, REP + TP, 0, 0, tiled=True)
    fresh_terms = fresh_terms.reshape(lax.axis_size(REP), lax.axis_size(TP), block_width)
    fresh_output = jnp.sum(fresh_terms.astype(jnp.float32), axis=1).astype(jnp.bfloat16)
    fresh_output = fresh_output.reshape(1, -1)
    attended = attend(queries, key_cache_slots, value_cache_slots, cache_lengths, fresh_output)
    return (master_new, first_new, second_new, attended)


def solution(mesh):
    fine = Mesh(mesh.devices.reshape(mesh.devices.shape[0], -1, 2, 2, 8), FINE_AXES)
    placed = (
        P("side", REP, TP),
        P("side", REP + TP, None),
        P(TP, REP),
        P(TP, REP),
        P(TP, REP),
        P(("side",) + REP, TP),
        P(("side",) + REP + TP, None),
        P(("side",) + REP + TP, None, None),
        P(("side",) + REP + TP, None, None),
        P(("side",) + REP + TP),
    )
    return jax.shard_map(
        local,
        mesh=fine,
        in_specs=placed,
        out_specs=(P(TP, REP), P(TP, REP), P(TP, REP), P(("side",) + REP + TP, None)),
        check_vma=False,
    )
```

```python
import functools

import jax
import jax.numpy as jnp
from jax import lax
from jax.experimental import pallas as pl
from jax.experimental.pallas import tpu as pltpu
from jax.sharding import Mesh
from jax.sharding import PartitionSpec as P

QUERY_HEADS = 64
KEY_VALUE_HEADS = 8
HEAD_SIZE = 128
STEP = 10


BETA_FIRST = 0.9
BETA_SECOND = 0.95
ADAM_EPSILON = 1e-08
LEARN_RATE = 0.001
DECAY_RATE = 0.1


def adamw(master, first_moment, second_moment, gradient):
    first_full = BETA_FIRST * first_moment.astype(jnp.float32) + (1.0 - BETA_FIRST) * gradient
    second_full = (
        BETA_SECOND * second_moment.astype(jnp.float32) + (1.0 - BETA_SECOND) * gradient * gradient
    )
    first_fix = 1.0 - BETA_FIRST**STEP
    second_fix = 1.0 - BETA_SECOND**STEP
    update = first_full / first_fix / (jnp.sqrt(second_full / second_fix) + ADAM_EPSILON)
    master_new = master - LEARN_RATE * (update + DECAY_RATE * master)
    return (master_new, first_full.astype(jnp.bfloat16), second_full.astype(jnp.bfloat16))


def attend(queries, key_cache_slots, value_cache_slots, cache_lengths, fresh_output):
    decode_row_count = queries.shape[0]
    slot_length = key_cache_slots.shape[1]
    query_groups = QUERY_HEADS // KEY_VALUE_HEADS
    query_head_rows = queries.reshape(decode_row_count, KEY_VALUE_HEADS, query_groups, HEAD_SIZE)
    stored_keys = key_cache_slots.reshape(decode_row_count, slot_length, KEY_VALUE_HEADS, HEAD_SIZE)
    stored_values = value_cache_slots.reshape(
        decode_row_count, slot_length, KEY_VALUE_HEADS, HEAD_SIZE
    )
    newest_keys = fresh_output[:, : KEY_VALUE_HEADS * HEAD_SIZE].reshape(
        decode_row_count, KEY_VALUE_HEADS, HEAD_SIZE
    )
    newest_values = fresh_output[:, KEY_VALUE_HEADS * HEAD_SIZE :].reshape(
        decode_row_count, KEY_VALUE_HEADS, HEAD_SIZE
    )
    score_scale = HEAD_SIZE ** (-0.5)
    scores = (
        jnp.einsum(
            "bkgd,blkd->bkgl", query_head_rows, stored_keys, preferred_element_type=jnp.float32
        )
        * score_scale
    )
    visible = jnp.arange(slot_length, dtype=jnp.int32)[None, :] < cache_lengths[:, None]
    scores = jnp.where(visible[:, None, None, :], scores, -1e30)
    self_score = (
        jnp.einsum(
            "zwai,zwi->zwa", query_head_rows, newest_keys, preferred_element_type=jnp.float32
        )
        * score_scale
    )
    highest = jnp.maximum(jnp.max(scores, axis=-1), self_score)
    weights = jnp.exp(scores - highest[..., None])
    own_weight = jnp.exp(self_score - highest)
    denominator = jnp.sum(weights, axis=-1) + own_weight
    probabilities = (weights / denominator[..., None]).astype(jnp.bfloat16)
    own_prob = (own_weight / denominator).astype(jnp.bfloat16)
    mixed = jnp.einsum(
        "bkgl,blkd->bkgd", probabilities, stored_values, preferred_element_type=jnp.float32
    )
    mixed = (
        mixed
        + own_prob.astype(jnp.float32)[..., None] * newest_values.astype(jnp.float32)[:, :, None, :]
    )
    return mixed.reshape(decode_row_count, QUERY_HEADS * HEAD_SIZE).astype(jnp.bfloat16)


FINE_AXES = ("side", "x", "core", "zhi", "y")
REP = ("x", "core")
TP = ("zhi", "y")


def swap_over(array, axis):
    return lax.ppermute(array, axis, [(0, 1), (1, 0)])


def shifted(array, axis, by):
    count = lax.axis_size(axis)
    return lax.ppermute(array, axis, [(i, (i + by) % count) for i in range(count)])


def around(array, axis, way):
    behind, ahead = shifted(array, axis, 1), shifted(array, axis, -1)
    across = shifted(behind if way == 1 else ahead, axis, way)
    return [array, behind, across, ahead]


VMEM = pl.BlockSpec(memory_space=pltpu.VMEM)
SMALL_KERNEL = pltpu.CompilerParams(vmem_limit_bytes=16 * 2**20)


def columns_kernel(grads, out):
    width = out.shape[2]
    for i in range(out.shape[0]):
        out[i] = grads[:, i * width : (i + 1) * width]


def columns_by_x(grads, x_count):
    shape = (x_count, grads.shape[0], grads.shape[1] // x_count)
    return pl.pallas_call(
        columns_kernel,
        out_shape=jax.ShapeDtypeStruct(shape, grads.dtype),
        in_specs=[VMEM],
        out_specs=VMEM,
        compiler_params=SMALL_KERNEL,
        name="columns",
    )(grads)


def copies_kernel(array, out, sems):
    copies = [
        pltpu.make_async_copy(array, out.at[i], sems.at[i]) for i in range(out.shape[0])
    ]
    for copy in copies:
        copy.start()
    for copy in copies:
        copy.wait()


def copies_of(array, count):
    return pl.pallas_call(
        copies_kernel,
        out_shape=jax.ShapeDtypeStruct((count, *array.shape), array.dtype),
        in_specs=[VMEM],
        out_specs=pl.BlockSpec(memory_space=pl.ANY),
        scratch_shapes=[pltpu.SemaphoreType.DMA((count,))],
        compiler_params=SMALL_KERNEL,
        name="copies",
    )(array)


def total_kernel(kept, received, out):
    out[...] = (kept[...] + received[: out.shape[0]].astype(jnp.float32)).astype(out.dtype)


def total_of(kept, received):
    return pl.pallas_call(
        total_kernel,
        out_shape=jax.ShapeDtypeStruct(kept.shape, received.dtype),
        in_specs=[VMEM, VMEM],
        out_specs=VMEM,
        compiler_params=SMALL_KERNEL,
        name="total",
    )(kept, received)


def quarters_kernel(terms, out):
    total = terms[0].astype(jnp.float32)
    for i in range(1, terms.shape[0]):
        total = total + terms[i].astype(jnp.float32)
    total = total.T.astype(out.dtype)
    for i in range(out.shape[0]):
        out[i] = total


def quarters_of(terms, count):
    _, width, lanes = terms.shape
    return pl.pallas_call(
        quarters_kernel,
        out_shape=jax.ShapeDtypeStruct((count, lanes, width), terms.dtype),
        in_specs=[VMEM],
        out_specs=VMEM,
        compiler_params=SMALL_KERNEL,
        name="quarters",
    )(terms)


def same_kernel(array, out):
    pass


def held(array):
    return pl.pallas_call(
        same_kernel,
        out_shape=jax.ShapeDtypeStruct(array.shape, array.dtype),
        in_specs=[pl.BlockSpec(memory_space=pl.ANY)],
        out_specs=pl.BlockSpec(memory_space=pl.ANY),
        input_output_aliases={0: 0},
        cost_estimate=pl.CostEstimate(flops=24 * 10**9, bytes_accessed=0, transcendentals=0),
        name="held",
    )(array)


def product_kernel(for_other, position, *refs):
    *inputs, grads, out = refs
    half, along, core = position[0], position[1], position[2]
    y_count, x_count, rows, _ = grads.shape
    half_rows = y_count * rows
    feature_count = inputs[0].shape[1]
    _, width, lanes = out.shape
    parts = feature_count // lanes
    column = 1 - core if for_other else core
    columns = pl.ds(pl.multiple_of(column * width, width), width)
    sources = [lax.rem(along - behind + x_count, x_count) for behind in range(x_count)]
    grads_rows = jnp.concatenate(
        [grads[y, source, :, columns] for source in sources for y in range(y_count)]
    )
    for blocks, place in ((inputs[:x_count], half), (inputs[x_count:], 1 - half)):
        inputs_rows = jnp.concatenate([block[:half_rows, :] for block in blocks])
        product = lax.dot_general(
            grads_rows,
            inputs_rows,
            (((0,), (0,)), ((), ())),
            preferred_element_type=jnp.float32,
        ).astype(out.dtype)
        for part in range(parts):
            out[place * parts + part] = product[:, part * lanes : (part + 1) * lanes]
    if for_other:
        decode_rows = inputs[0].shape[0] - half_rows
        for part in range(parts):
            for block, source in zip(inputs[:x_count], sources):
                start = (part * x_count + source) * decode_rows
                target = pl.ds(pl.multiple_of(start, decode_rows), decode_rows)
                out[2 * parts, target, :] = block[half_rows:, part * lanes : (part + 1) * lanes]


def products(for_other, inputs, grads, width, lanes):
    feature_count = inputs[0].shape[1]
    position = jnp.stack([lax.axis_index(axis) for axis in ("zhi", "x", "core")]).astype(jnp.int32)
    y_count, x_count, rows, _ = grads.shape
    blocks = 2 * feature_count // lanes + for_other
    dtype = jnp.bfloat16 if for_other else jnp.float32
    return pl.pallas_call(
        functools.partial(product_kernel, for_other),
        out_shape=jax.ShapeDtypeStruct((blocks, width, lanes), dtype),
        in_specs=[pl.BlockSpec(memory_space=pltpu.SMEM)]
        + [pl.BlockSpec(memory_space=pltpu.VMEM)] * (len(inputs) + 1),
        out_specs=pl.BlockSpec(memory_space=pltpu.VMEM),
        compiler_params=pltpu.CompilerParams(vmem_limit_bytes=32 * 2**20),
        cost_estimate=pl.CostEstimate(
            flops=4 * feature_count * y_count * x_count * rows * width,
            bytes_accessed=7 * 2**20,
            transcendentals=0,
        ),
        name="products_other" if for_other else "products_own",
    )(position, *inputs, grads)


def local(
    learn_inputs,
    learn_grads,
    kv_master,
    first_moment,
    second_moment,
    decode_inputs,
    queries,
    key_cache_slots,
    value_cache_slots,
    cache_lengths,
):
    core, half = lax.axis_index("core"), lax.axis_index("zhi")
    x_count, side_count = lax.axis_size("x"), lax.axis_size("side")
    feature_count = learn_inputs.shape[2]
    block_width = kv_master.shape[1]
    quarter = feature_count // side_count

    row_halves = learn_inputs[0].reshape(2, -1, feature_count)
    received = swap_over(jnp.where(half == 0, row_halves[1], row_halves[0]), "zhi")
    kept = jnp.concatenate([jnp.where(half == 0, row_halves[0], row_halves[1]), decode_inputs])

    columns = columns_by_x(learn_grads[0], x_count)
    piece = lax.all_to_all(columns, "x", 0, 0, tiled=True)
    piece, kept = lax.optimization_barrier((piece, kept))
    y_count = lax.axis_size("y")
    grads_all = lax.all_to_all(copies_of(piece, y_count), "y", 0, 0)
    behind, ahead = shifted(kept, "x", 1), shifted(kept, "x", -1)
    received = held(received)
    ahead, received = lax.optimization_barrier((ahead, received))
    inputs = [kept, behind, shifted(behind, "x", 1), ahead] + around(received, "x", -1)

    sent = products(True, inputs, grads_all, block_width, quarter)
    sent_back = swap_over(sent, "core")
    kept_sum = products(False, inputs, grads_all, block_width, quarter)
    over_rep = total_of(kept_sum, sent_back)
    decode_of_core = [
        jnp.concatenate(jnp.split(array[-1], side_count), axis=1).reshape(x_count, -1, feature_count)
        for array in (sent, sent_back)
    ]
    decode_rows = jnp.where(
        core == 0, jnp.stack(decode_of_core, 1), jnp.stack(decode_of_core[::-1], 1)
    ).reshape(-1, feature_count)
    terms = lax.all_to_all(over_rep, ("zhi", "side"), 0, 0, tiled=True)
    gradient = lax.all_to_all(quarters_of(terms, side_count), "side", 0, 0, tiled=True)
    gradient = gradient.reshape(feature_count, block_width).astype(jnp.float32)
    master_new, first_new, second_new = adamw(kv_master, first_moment, second_moment, gradient)
    rounded_weights = master_new.astype(jnp.bfloat16)
    partial_fresh = jnp.dot(decode_rows, rounded_weights, preferred_element_type=jnp.float32)
    partial_fresh = partial_fresh.astype(jnp.bfloat16).reshape(-1, 2, block_width // 2)
    fresh_terms = lax.all_to_all(partial_fresh, REP + TP, 0, 0, tiled=True)
    fresh_terms = fresh_terms.reshape(lax.axis_size(REP), lax.axis_size(TP), block_width)
    fresh_output = jnp.sum(fresh_terms.astype(jnp.float32), axis=1).astype(jnp.bfloat16)
    fresh_output = fresh_output.reshape(1, -1)
    attended = attend(queries, key_cache_slots, value_cache_slots, cache_lengths, fresh_output)
    return (master_new, first_new, second_new, attended)


def solution(mesh):
    fine = Mesh(mesh.devices.reshape(mesh.devices.shape[0], -1, 2, 2, 8), FINE_AXES)
    placed = (
        P("side", REP, TP),
        P("side", REP + TP, None),
        P(TP, REP),
        P(TP, REP),
        P(TP, REP),
        P(("side",) + REP, TP),
        P(("side",) + REP + TP, None),
        P(("side",) + REP + TP, None, None),
        P(("side",) + REP + TP, None, None),
        P(("side",) + REP + TP),
    )
    return jax.shard_map(
        local,
        mesh=fine,
        in_specs=placed,
        out_specs=(P(TP, REP), P(TP, REP), P(TP, REP), P(("side",) + REP + TP, None)),
        check_vma=False,
    )
```

```python
import functools

import jax
import jax.numpy as jnp
from jax import lax
from jax.experimental import pallas as pl
from jax.experimental.pallas import tpu as pltpu
from jax.sharding import Mesh
from jax.sharding import PartitionSpec as P

QUERY_HEADS = 64
KEY_VALUE_HEADS = 8
HEAD_SIZE = 128
STEP = 10


BETA_FIRST = 0.9
BETA_SECOND = 0.95
ADAM_EPSILON = 1e-08
LEARN_RATE = 0.001
DECAY_RATE = 0.1


def adamw(master, first_moment, second_moment, gradient):
    first_full = BETA_FIRST * first_moment.astype(jnp.float32) + (1.0 - BETA_FIRST) * gradient
    second_full = (
        BETA_SECOND * second_moment.astype(jnp.float32) + (1.0 - BETA_SECOND) * gradient * gradient
    )
    first_fix = 1.0 - BETA_FIRST**STEP
    second_fix = 1.0 - BETA_SECOND**STEP
    update = first_full / first_fix / (jnp.sqrt(second_full / second_fix) + ADAM_EPSILON)
    master_new = master - LEARN_RATE * (update + DECAY_RATE * master)
    return (master_new, first_full.astype(jnp.bfloat16), second_full.astype(jnp.bfloat16))


def attend(queries, key_cache_slots, value_cache_slots, cache_lengths, fresh_output):
    decode_row_count = queries.shape[0]
    slot_length = key_cache_slots.shape[1]
    query_groups = QUERY_HEADS // KEY_VALUE_HEADS
    query_head_rows = queries.reshape(decode_row_count, KEY_VALUE_HEADS, query_groups, HEAD_SIZE)
    stored_keys = key_cache_slots.reshape(decode_row_count, slot_length, KEY_VALUE_HEADS, HEAD_SIZE)
    stored_values = value_cache_slots.reshape(
        decode_row_count, slot_length, KEY_VALUE_HEADS, HEAD_SIZE
    )
    newest_keys = fresh_output[:, : KEY_VALUE_HEADS * HEAD_SIZE].reshape(
        decode_row_count, KEY_VALUE_HEADS, HEAD_SIZE
    )
    newest_values = fresh_output[:, KEY_VALUE_HEADS * HEAD_SIZE :].reshape(
        decode_row_count, KEY_VALUE_HEADS, HEAD_SIZE
    )
    score_scale = HEAD_SIZE ** (-0.5)
    scores = (
        jnp.einsum(
            "bkgd,blkd->bkgl", query_head_rows, stored_keys, preferred_element_type=jnp.float32
        )
        * score_scale
    )
    visible = jnp.arange(slot_length, dtype=jnp.int32)[None, :] < cache_lengths[:, None]
    scores = jnp.where(visible[:, None, None, :], scores, -1e30)
    self_score = (
        jnp.einsum(
            "zwai,zwi->zwa", query_head_rows, newest_keys, preferred_element_type=jnp.float32
        )
        * score_scale
    )
    highest = jnp.maximum(jnp.max(scores, axis=-1), self_score)
    weights = jnp.exp(scores - highest[..., None])
    own_weight = jnp.exp(self_score - highest)
    denominator = jnp.sum(weights, axis=-1) + own_weight
    probabilities = (weights / denominator[..., None]).astype(jnp.bfloat16)
    own_prob = (own_weight / denominator).astype(jnp.bfloat16)
    mixed = jnp.einsum(
        "bkgl,blkd->bkgd", probabilities, stored_values, preferred_element_type=jnp.float32
    )
    mixed = (
        mixed
        + own_prob.astype(jnp.float32)[..., None] * newest_values.astype(jnp.float32)[:, :, None, :]
    )
    return mixed.reshape(decode_row_count, QUERY_HEADS * HEAD_SIZE).astype(jnp.bfloat16)


FINE_AXES = ("side", "x", "core", "zhi", "y")
REP = ("x", "core")
TP = ("zhi", "y")


def swap_over(array, axis):
    return lax.ppermute(array, axis, [(0, 1), (1, 0)])


def shifted(array, axis, by):
    count = lax.axis_size(axis)
    return lax.ppermute(array, axis, [(i, (i + by) % count) for i in range(count)])


def around(array, axis, way):
    behind, ahead = shifted(array, axis, 1), shifted(array, axis, -1)
    across = shifted(behind if way == 1 else ahead, axis, way)
    return [array, behind, across, ahead]


VMEM = pl.BlockSpec(memory_space=pltpu.VMEM)
HBM = pl.BlockSpec(memory_space=pltpu.HBM)
SMALL_KERNEL = pltpu.CompilerParams(vmem_limit_bytes=16 * 2**20)
HBM_KERNEL = pltpu.CompilerParams(vmem_limit_bytes=60 * 2**20)


def columns_kernel(grads, out, sems):
    width = out.shape[2]
    copies = [
        pltpu.make_async_copy(grads.at[:, pl.ds(i * width, width)], out.at[i], sems.at[i])
        for i in range(out.shape[0])
    ]
    for copy in copies:
        copy.start()
    for copy in copies:
        copy.wait()


def columns_by_x(grads, x_count):
    shape = (x_count, grads.shape[0], grads.shape[1] // x_count)
    return pl.pallas_call(
        columns_kernel,
        out_shape=jax.ShapeDtypeStruct(shape, grads.dtype),
        in_specs=[HBM],
        out_specs=HBM,
        scratch_shapes=[pltpu.SemaphoreType.DMA((x_count,))],
        compiler_params=HBM_KERNEL,
        name="columns",
    )(grads)


def copies_kernel(array, out, sems):
    copies = [
        pltpu.make_async_copy(array, out.at[i], sems.at[i]) for i in range(out.shape[0])
    ]
    for copy in copies:
        copy.start()
    for copy in copies:
        copy.wait()


def copies_of(array, count):
    return pl.pallas_call(
        copies_kernel,
        out_shape=jax.ShapeDtypeStruct((count, *array.shape), array.dtype),
        in_specs=[VMEM],
        out_specs=HBM,
        scratch_shapes=[pltpu.SemaphoreType.DMA((count,))],
        compiler_params=HBM_KERNEL,
        name="copies",
    )(array)


def total_kernel(kept, received, out, total, sem):
    total[...] = (kept[...] + received[: total.shape[0]].astype(jnp.float32)).astype(total.dtype)
    copy = pltpu.make_async_copy(total, out, sem)
    copy.start()
    copy.wait()


def total_of(kept, received):
    return pl.pallas_call(
        total_kernel,
        out_shape=jax.ShapeDtypeStruct(kept.shape, received.dtype),
        in_specs=[VMEM, VMEM],
        out_specs=HBM,
        scratch_shapes=[pltpu.VMEM(kept.shape, received.dtype), pltpu.SemaphoreType.DMA],
        compiler_params=SMALL_KERNEL,
        name="total",
    )(kept, received)


def quarters_kernel(terms, out):
    total = terms[0].astype(jnp.float32)
    for i in range(1, terms.shape[0]):
        total = total + terms[i].astype(jnp.float32)
    total = total.T.astype(out.dtype)
    for i in range(out.shape[0]):
        out[i] = total


def quarters_of(terms, count):
    _, width, lanes = terms.shape
    return pl.pallas_call(
        quarters_kernel,
        out_shape=jax.ShapeDtypeStruct((count, lanes, width), terms.dtype),
        in_specs=[VMEM],
        out_specs=VMEM,
        compiler_params=SMALL_KERNEL,
        name="quarters",
    )(terms)


def same_kernel(array, out):
    pass


def held(array):
    return pl.pallas_call(
        same_kernel,
        out_shape=jax.ShapeDtypeStruct(array.shape, array.dtype),
        in_specs=[pl.BlockSpec(memory_space=pl.ANY)],
        out_specs=pl.BlockSpec(memory_space=pl.ANY),
        input_output_aliases={0: 0},
        cost_estimate=pl.CostEstimate(flops=26 * 10**9, bytes_accessed=0, transcendentals=0),
        name="held",
    )(array)


def product_kernel(for_other, position, *refs):
    *inputs, grads, out = refs
    half, along, core = position[0], position[1], position[2]
    y_count, x_count, rows, _ = grads.shape
    half_rows = y_count * rows
    feature_count = inputs[0].shape[1]
    _, width, lanes = out.shape
    parts = feature_count // lanes
    column = 1 - core if for_other else core
    columns = pl.ds(pl.multiple_of(column * width, width), width)
    sources = [lax.rem(along - behind + x_count, x_count) for behind in range(x_count)]
    grads_rows = jnp.concatenate(
        [grads[y, source, :, columns] for source in sources for y in range(y_count)]
    )
    for blocks, place in ((inputs[:x_count], half), (inputs[x_count:], 1 - half)):
        inputs_rows = jnp.concatenate([block[:half_rows, :] for block in blocks])
        product = lax.dot_general(
            grads_rows,
            inputs_rows,
            (((0,), (0,)), ((), ())),
            preferred_element_type=jnp.float32,
        ).astype(out.dtype)
        for part in range(parts):
            out[place * parts + part] = product[:, part * lanes : (part + 1) * lanes]
    if for_other:
        decode_rows = inputs[0].shape[0] - half_rows
        for part in range(parts):
            for block, source in zip(inputs[:x_count], sources):
                start = (part * x_count + source) * decode_rows
                target = pl.ds(pl.multiple_of(start, decode_rows), decode_rows)
                out[2 * parts, target, :] = block[half_rows:, part * lanes : (part + 1) * lanes]


def products(for_other, inputs, grads, width, lanes):
    feature_count = inputs[0].shape[1]
    position = jnp.stack([lax.axis_index(axis) for axis in ("zhi", "x", "core")]).astype(jnp.int32)
    y_count, x_count, rows, _ = grads.shape
    blocks = 2 * feature_count // lanes + for_other
    dtype = jnp.bfloat16 if for_other else jnp.float32
    return pl.pallas_call(
        functools.partial(product_kernel, for_other),
        out_shape=jax.ShapeDtypeStruct((blocks, width, lanes), dtype),
        in_specs=[pl.BlockSpec(memory_space=pltpu.SMEM)]
        + [pl.BlockSpec(memory_space=pltpu.VMEM)] * (len(inputs) + 1),
        out_specs=pl.BlockSpec(memory_space=pltpu.VMEM),
        compiler_params=pltpu.CompilerParams(vmem_limit_bytes=32 * 2**20),
        cost_estimate=pl.CostEstimate(
            flops=4 * feature_count * y_count * x_count * rows * width,
            bytes_accessed=7 * 2**20,
            transcendentals=0,
        ),
        name="products_other" if for_other else "products_own",
    )(position, *inputs, grads)


def local(
    learn_inputs,
    learn_grads,
    kv_master,
    first_moment,
    second_moment,
    decode_inputs,
    queries,
    key_cache_slots,
    value_cache_slots,
    cache_lengths,
):
    core, half = lax.axis_index("core"), lax.axis_index("zhi")
    x_count, side_count = lax.axis_size("x"), lax.axis_size("side")
    feature_count = learn_inputs.shape[2]
    block_width = kv_master.shape[1]
    quarter = feature_count // side_count

    row_halves = learn_inputs[0].reshape(2, -1, feature_count)
    received = swap_over(jnp.where(half == 0, row_halves[1], row_halves[0]), "zhi")
    kept = jnp.concatenate([jnp.where(half == 0, row_halves[0], row_halves[1]), decode_inputs])

    columns = columns_by_x(learn_grads[0], x_count)
    piece = lax.all_to_all(columns, "x", 0, 0, tiled=True)
    piece, kept = lax.optimization_barrier((piece, kept))
    y_count = lax.axis_size("y")
    grads_all = lax.all_to_all(copies_of(piece, y_count), "y", 0, 0)
    behind, ahead = shifted(kept, "x", 1), shifted(kept, "x", -1)
    received = held(received)
    ahead, received = lax.optimization_barrier((ahead, received))
    inputs = [kept, behind, shifted(behind, "x", 1), ahead] + around(received, "x", -1)

    sent = products(True, inputs, grads_all, block_width, quarter)
    sent_back = swap_over(sent, "core")
    kept_sum = products(False, inputs, grads_all, block_width, quarter)
    over_rep = total_of(kept_sum, sent_back)
    decode_of_core = [
        jnp.concatenate(jnp.split(array[-1], side_count), axis=1).reshape(x_count, -1, feature_count)
        for array in (sent, sent_back)
    ]
    decode_rows = jnp.where(
        core == 0, jnp.stack(decode_of_core, 1), jnp.stack(decode_of_core[::-1], 1)
    ).reshape(-1, feature_count)
    terms = lax.all_to_all(over_rep, ("zhi", "side"), 0, 0, tiled=True)
    gradient = lax.all_to_all(quarters_of(terms, side_count), "side", 0, 0, tiled=True)
    gradient = gradient.reshape(feature_count, block_width).astype(jnp.float32)
    master_new, first_new, second_new = adamw(kv_master, first_moment, second_moment, gradient)
    rounded_weights = master_new.astype(jnp.bfloat16)
    partial_fresh = jnp.dot(decode_rows, rounded_weights, preferred_element_type=jnp.float32)
    partial_fresh = partial_fresh.astype(jnp.bfloat16).reshape(-1, 2, block_width // 2)
    fresh_terms = lax.all_to_all(partial_fresh, REP + TP, 0, 0, tiled=True)
    fresh_terms = fresh_terms.reshape(lax.axis_size(REP), lax.axis_size(TP), block_width)
    fresh_output = jnp.sum(fresh_terms.astype(jnp.float32), axis=1).astype(jnp.bfloat16)
    fresh_output = fresh_output.reshape(1, -1)
    attended = attend(queries, key_cache_slots, value_cache_slots, cache_lengths, fresh_output)
    return (master_new, first_new, second_new, attended)


def solution(mesh):
    fine = Mesh(mesh.devices.reshape(mesh.devices.shape[0], -1, 2, 2, 8), FINE_AXES)
    placed = (
        P("side", REP, TP),
        P("side", REP + TP, None),
        P(TP, REP),
        P(TP, REP),
        P(TP, REP),
        P(("side",) + REP, TP),
        P(("side",) + REP + TP, None),
        P(("side",) + REP + TP, None, None),
        P(("side",) + REP + TP, None, None),
        P(("side",) + REP + TP),
    )
    return jax.shard_map(
        local,
        mesh=fine,
        in_specs=placed,
        out_specs=(P(TP, REP), P(TP, REP), P(TP, REP), P(("side",) + REP + TP, None)),
        check_vma=False,
    )
```

```python
import functools

import jax
import jax.numpy as jnp
from jax import lax
from jax.experimental import pallas as pl
from jax.experimental.pallas import tpu as pltpu
from jax.sharding import Mesh
from jax.sharding import PartitionSpec as P

QUERY_HEADS = 64
KEY_VALUE_HEADS = 8
HEAD_SIZE = 128
STEP = 10


BETA_FIRST = 0.9
BETA_SECOND = 0.95
ADAM_EPSILON = 1e-08
LEARN_RATE = 0.001
DECAY_RATE = 0.1


def adamw(master, first_moment, second_moment, gradient):
    first_full = BETA_FIRST * first_moment.astype(jnp.float32) + (1.0 - BETA_FIRST) * gradient
    second_full = (
        BETA_SECOND * second_moment.astype(jnp.float32) + (1.0 - BETA_SECOND) * gradient * gradient
    )
    first_fix = 1.0 - BETA_FIRST**STEP
    second_fix = 1.0 - BETA_SECOND**STEP
    update = first_full / first_fix / (jnp.sqrt(second_full / second_fix) + ADAM_EPSILON)
    master_new = master - LEARN_RATE * (update + DECAY_RATE * master)
    return (master_new, first_full.astype(jnp.bfloat16), second_full.astype(jnp.bfloat16))


def attend(queries, key_cache_slots, value_cache_slots, cache_lengths, fresh_output):
    decode_row_count = queries.shape[0]
    slot_length = key_cache_slots.shape[1]
    query_groups = QUERY_HEADS // KEY_VALUE_HEADS
    query_head_rows = queries.reshape(decode_row_count, KEY_VALUE_HEADS, query_groups, HEAD_SIZE)
    stored_keys = key_cache_slots.reshape(decode_row_count, slot_length, KEY_VALUE_HEADS, HEAD_SIZE)
    stored_values = value_cache_slots.reshape(
        decode_row_count, slot_length, KEY_VALUE_HEADS, HEAD_SIZE
    )
    newest_keys = fresh_output[:, : KEY_VALUE_HEADS * HEAD_SIZE].reshape(
        decode_row_count, KEY_VALUE_HEADS, HEAD_SIZE
    )
    newest_values = fresh_output[:, KEY_VALUE_HEADS * HEAD_SIZE :].reshape(
        decode_row_count, KEY_VALUE_HEADS, HEAD_SIZE
    )
    score_scale = HEAD_SIZE ** (-0.5)
    scores = (
        jnp.einsum(
            "bkgd,blkd->bkgl", query_head_rows, stored_keys, preferred_element_type=jnp.float32
        )
        * score_scale
    )
    visible = jnp.arange(slot_length, dtype=jnp.int32)[None, :] < cache_lengths[:, None]
    scores = jnp.where(visible[:, None, None, :], scores, -1e30)
    self_score = (
        jnp.einsum(
            "zwai,zwi->zwa", query_head_rows, newest_keys, preferred_element_type=jnp.float32
        )
        * score_scale
    )
    highest = jnp.maximum(jnp.max(scores, axis=-1), self_score)
    weights = jnp.exp(scores - highest[..., None])
    own_weight = jnp.exp(self_score - highest)
    denominator = jnp.sum(weights, axis=-1) + own_weight
    probabilities = (weights / denominator[..., None]).astype(jnp.bfloat16)
    own_prob = (own_weight / denominator).astype(jnp.bfloat16)
    mixed = jnp.einsum(
        "bkgl,blkd->bkgd", probabilities, stored_values, preferred_element_type=jnp.float32
    )
    mixed = (
        mixed
        + own_prob.astype(jnp.float32)[..., None] * newest_values.astype(jnp.float32)[:, :, None, :]
    )
    return mixed.reshape(decode_row_count, QUERY_HEADS * HEAD_SIZE).astype(jnp.bfloat16)


FINE_AXES = ("side", "x", "core", "zhi", "y")
REP = ("x", "core")
TP = ("zhi", "y")


def swap_over(array, axis):
    return lax.ppermute(array, axis, [(0, 1), (1, 0)])


def shifted(array, axis, by):
    count = lax.axis_size(axis)
    return lax.ppermute(array, axis, [(i, (i + by) % count) for i in range(count)])


def around(array, axis, way):
    behind, ahead = shifted(array, axis, 1), shifted(array, axis, -1)
    across = shifted(behind if way == 1 else ahead, axis, way)
    return [array, behind, across, ahead]


VMEM = pl.BlockSpec(memory_space=pltpu.VMEM)
HBM = pl.BlockSpec(memory_space=pltpu.HBM)
SMALL_KERNEL = pltpu.CompilerParams(vmem_limit_bytes=16 * 2**20)


def columns_kernel(grads, out):
    width = out.shape[2]
    for i in range(out.shape[0]):
        out[i] = grads[:, i * width : (i + 1) * width]


def columns_by_x(grads, x_count):
    shape = (x_count, grads.shape[0], grads.shape[1] // x_count)
    return pl.pallas_call(
        columns_kernel,
        out_shape=jax.ShapeDtypeStruct(shape, grads.dtype),
        in_specs=[VMEM],
        out_specs=VMEM,
        compiler_params=SMALL_KERNEL,
        name="columns",
    )(grads)


def total_kernel(kept, received, out, total, sem):
    total[...] = (kept[...] + received[: total.shape[0]].astype(jnp.float32)).astype(total.dtype)
    copy = pltpu.make_async_copy(total, out, sem)
    copy.start()
    copy.wait()


def total_of(kept, received):
    return pl.pallas_call(
        total_kernel,
        out_shape=jax.ShapeDtypeStruct(kept.shape, received.dtype),
        in_specs=[VMEM, VMEM],
        out_specs=HBM,
        scratch_shapes=[pltpu.VMEM(kept.shape, received.dtype), pltpu.SemaphoreType.DMA],
        compiler_params=SMALL_KERNEL,
        name="total",
    )(kept, received)


def quarters_kernel(terms, out):
    total = terms[0].astype(jnp.float32)
    for i in range(1, terms.shape[0]):
        total = total + terms[i].astype(jnp.float32)
    total = total.T.astype(out.dtype)
    for i in range(out.shape[0]):
        out[i] = total


def quarters_of(terms, count):
    _, width, lanes = terms.shape
    return pl.pallas_call(
        quarters_kernel,
        out_shape=jax.ShapeDtypeStruct((count, lanes, width), terms.dtype),
        in_specs=[VMEM],
        out_specs=VMEM,
        compiler_params=SMALL_KERNEL,
        name="quarters",
    )(terms)


def same_kernel(array, out):
    pass


def held(array):
    return pl.pallas_call(
        same_kernel,
        out_shape=jax.ShapeDtypeStruct(array.shape, array.dtype),
        in_specs=[pl.BlockSpec(memory_space=pl.ANY)],
        out_specs=pl.BlockSpec(memory_space=pl.ANY),
        input_output_aliases={0: 0},
        cost_estimate=pl.CostEstimate(flops=26 * 10**9, bytes_accessed=0, transcendentals=0),
        name="held",
    )(array)


def product_kernel(for_other, position, *refs):
    *inputs, grads, out = refs
    half, along, core = position[0], position[1], position[2]
    y_count, x_count, rows, _ = grads.shape
    half_rows = y_count * rows
    feature_count = inputs[0].shape[1]
    _, width, lanes = out.shape
    parts = feature_count // lanes
    column = 1 - core if for_other else core
    columns = pl.ds(pl.multiple_of(column * width, width), width)
    sources = [lax.rem(along - behind + x_count, x_count) for behind in range(x_count)]
    grads_rows = jnp.concatenate(
        [grads[y, source, :, columns] for source in sources for y in range(y_count)]
    )
    for blocks, place in ((inputs[:x_count], half), (inputs[x_count:], 1 - half)):
        inputs_rows = jnp.concatenate([block[:half_rows, :] for block in blocks])
        product = lax.dot_general(
            grads_rows,
            inputs_rows,
            (((0,), (0,)), ((), ())),
            preferred_element_type=jnp.float32,
        ).astype(out.dtype)
        for part in range(parts):
            out[place * parts + part] = product[:, part * lanes : (part + 1) * lanes]
    if for_other:
        decode_rows = inputs[0].shape[0] - half_rows
        for part in range(parts):
            for block, source in zip(inputs[:x_count], sources):
                start = (part * x_count + source) * decode_rows
                target = pl.ds(pl.multiple_of(start, decode_rows), decode_rows)
                out[2 * parts, target, :] = block[half_rows:, part * lanes : (part + 1) * lanes]


def products(for_other, inputs, grads, width, lanes):
    feature_count = inputs[0].shape[1]
    position = jnp.stack([lax.axis_index(axis) for axis in ("zhi", "x", "core")]).astype(jnp.int32)
    y_count, x_count, rows, _ = grads.shape
    blocks = 2 * feature_count // lanes + for_other
    dtype = jnp.bfloat16 if for_other else jnp.float32
    return pl.pallas_call(
        functools.partial(product_kernel, for_other),
        out_shape=jax.ShapeDtypeStruct((blocks, width, lanes), dtype),
        in_specs=[pl.BlockSpec(memory_space=pltpu.SMEM)]
        + [pl.BlockSpec(memory_space=pltpu.VMEM)] * (len(inputs) + 1),
        out_specs=pl.BlockSpec(memory_space=pltpu.VMEM),
        compiler_params=pltpu.CompilerParams(vmem_limit_bytes=32 * 2**20),
        cost_estimate=pl.CostEstimate(
            flops=4 * feature_count * y_count * x_count * rows * width,
            bytes_accessed=7 * 2**20,
            transcendentals=0,
        ),
        name="products_other" if for_other else "products_own",
    )(position, *inputs, grads)


def local(
    learn_inputs,
    learn_grads,
    kv_master,
    first_moment,
    second_moment,
    decode_inputs,
    queries,
    key_cache_slots,
    value_cache_slots,
    cache_lengths,
):
    core, half = lax.axis_index("core"), lax.axis_index("zhi")
    x_count, side_count = lax.axis_size("x"), lax.axis_size("side")
    feature_count = learn_inputs.shape[2]
    block_width = kv_master.shape[1]
    quarter = feature_count // side_count

    row_halves = learn_inputs[0].reshape(2, -1, feature_count)
    received = swap_over(jnp.where(half == 0, row_halves[1], row_halves[0]), "zhi")
    kept = jnp.concatenate([jnp.where(half == 0, row_halves[0], row_halves[1]), decode_inputs])

    columns = columns_by_x(learn_grads[0], x_count)
    piece = lax.all_to_all(columns, "x", 0, 0, tiled=True)
    piece, kept = lax.optimization_barrier((piece, kept))
    y_count = lax.axis_size("y")
    copies = jnp.broadcast_to(piece[None], (y_count, *piece.shape))
    grads_all = lax.all_to_all(copies, "y", 0, 0)
    behind, ahead = shifted(kept, "x", 1), shifted(kept, "x", -1)
    received = held(received)
    ahead, received = lax.optimization_barrier((ahead, received))
    inputs = [kept, behind, shifted(behind, "x", 1), ahead] + around(received, "x", -1)

    sent = products(True, inputs, grads_all, block_width, quarter)
    sent_back = swap_over(sent, "core")
    kept_sum = products(False, inputs, grads_all, block_width, quarter)
    over_rep = total_of(kept_sum, sent_back)
    decode_of_core = [
        jnp.concatenate(jnp.split(array[-1], side_count), axis=1).reshape(x_count, -1, feature_count)
        for array in (sent, sent_back)
    ]
    decode_rows = jnp.where(
        core == 0, jnp.stack(decode_of_core, 1), jnp.stack(decode_of_core[::-1], 1)
    ).reshape(-1, feature_count)
    terms = lax.all_to_all(over_rep, ("zhi", "side"), 0, 0, tiled=True)
    gradient = lax.all_to_all(quarters_of(terms, side_count), "side", 0, 0, tiled=True)
    gradient = gradient.reshape(feature_count, block_width).astype(jnp.float32)
    master_new, first_new, second_new = adamw(kv_master, first_moment, second_moment, gradient)
    rounded_weights = master_new.astype(jnp.bfloat16)
    partial_fresh = jnp.dot(decode_rows, rounded_weights, preferred_element_type=jnp.float32)
    partial_fresh = partial_fresh.astype(jnp.bfloat16).reshape(-1, 2, block_width // 2)
    fresh_terms = lax.all_to_all(partial_fresh, REP + TP, 0, 0, tiled=True)
    fresh_terms = fresh_terms.reshape(lax.axis_size(REP), lax.axis_size(TP), block_width)
    fresh_output = jnp.sum(fresh_terms.astype(jnp.float32), axis=1).astype(jnp.bfloat16)
    fresh_output = fresh_output.reshape(1, -1)
    attended = attend(queries, key_cache_slots, value_cache_slots, cache_lengths, fresh_output)
    return (master_new, first_new, second_new, attended)


def solution(mesh):
    fine = Mesh(mesh.devices.reshape(mesh.devices.shape[0], -1, 2, 2, 8), FINE_AXES)
    placed = (
        P("side", REP, TP),
        P("side", REP + TP, None),
        P(TP, REP),
        P(TP, REP),
        P(TP, REP),
        P(("side",) + REP, TP),
        P(("side",) + REP + TP, None),
        P(("side",) + REP + TP, None, None),
        P(("side",) + REP + TP, None, None),
        P(("side",) + REP + TP),
    )
    return jax.shard_map(
        local,
        mesh=fine,
        in_specs=placed,
        out_specs=(P(TP, REP), P(TP, REP), P(TP, REP), P(("side",) + REP + TP, None)),
        check_vma=False,
    )
```

```python
import functools

import jax
import jax.numpy as jnp
from jax import lax
from jax.experimental import pallas as pl
from jax.experimental.pallas import tpu as pltpu
from jax.sharding import Mesh
from jax.sharding import PartitionSpec as P

QUERY_HEADS = 64
KEY_VALUE_HEADS = 8
HEAD_SIZE = 128
STEP = 10


BETA_FIRST = 0.9
BETA_SECOND = 0.95
ADAM_EPSILON = 1e-08
LEARN_RATE = 0.001
DECAY_RATE = 0.1


def adamw(master, first_moment, second_moment, gradient):
    first_full = BETA_FIRST * first_moment.astype(jnp.float32) + (1.0 - BETA_FIRST) * gradient
    second_full = (
        BETA_SECOND * second_moment.astype(jnp.float32) + (1.0 - BETA_SECOND) * gradient * gradient
    )
    first_fix = 1.0 - BETA_FIRST**STEP
    second_fix = 1.0 - BETA_SECOND**STEP
    update = first_full / first_fix / (jnp.sqrt(second_full / second_fix) + ADAM_EPSILON)
    master_new = master - LEARN_RATE * (update + DECAY_RATE * master)
    return (master_new, first_full.astype(jnp.bfloat16), second_full.astype(jnp.bfloat16))


def attend(queries, key_cache_slots, value_cache_slots, cache_lengths, fresh_output):
    decode_row_count = queries.shape[0]
    slot_length = key_cache_slots.shape[1]
    query_groups = QUERY_HEADS // KEY_VALUE_HEADS
    query_head_rows = queries.reshape(decode_row_count, KEY_VALUE_HEADS, query_groups, HEAD_SIZE)
    stored_keys = key_cache_slots.reshape(decode_row_count, slot_length, KEY_VALUE_HEADS, HEAD_SIZE)
    stored_values = value_cache_slots.reshape(
        decode_row_count, slot_length, KEY_VALUE_HEADS, HEAD_SIZE
    )
    newest_keys = fresh_output[:, : KEY_VALUE_HEADS * HEAD_SIZE].reshape(
        decode_row_count, KEY_VALUE_HEADS, HEAD_SIZE
    )
    newest_values = fresh_output[:, KEY_VALUE_HEADS * HEAD_SIZE :].reshape(
        decode_row_count, KEY_VALUE_HEADS, HEAD_SIZE
    )
    score_scale = HEAD_SIZE ** (-0.5)
    scores = (
        jnp.einsum(
            "bkgd,blkd->bkgl", query_head_rows, stored_keys, preferred_element_type=jnp.float32
        )
        * score_scale
    )
    visible = jnp.arange(slot_length, dtype=jnp.int32)[None, :] < cache_lengths[:, None]
    scores = jnp.where(visible[:, None, None, :], scores, -1e30)
    self_score = (
        jnp.einsum(
            "zwai,zwi->zwa", query_head_rows, newest_keys, preferred_element_type=jnp.float32
        )
        * score_scale
    )
    highest = jnp.maximum(jnp.max(scores, axis=-1), self_score)
    weights = jnp.exp(scores - highest[..., None])
    own_weight = jnp.exp(self_score - highest)
    denominator = jnp.sum(weights, axis=-1) + own_weight
    probabilities = (weights / denominator[..., None]).astype(jnp.bfloat16)
    own_prob = (own_weight / denominator).astype(jnp.bfloat16)
    mixed = jnp.einsum(
        "bkgl,blkd->bkgd", probabilities, stored_values, preferred_element_type=jnp.float32
    )
    mixed = (
        mixed
        + own_prob.astype(jnp.float32)[..., None] * newest_values.astype(jnp.float32)[:, :, None, :]
    )
    return mixed.reshape(decode_row_count, QUERY_HEADS * HEAD_SIZE).astype(jnp.bfloat16)


FINE_AXES = ("side", "x", "core", "zhi", "y")
REP = ("x", "core")
TP = ("zhi", "y")


def swap_over(array, axis):
    return lax.ppermute(array, axis, [(0, 1), (1, 0)])


def shifted(array, axis, by):
    count = lax.axis_size(axis)
    return lax.ppermute(array, axis, [(i, (i + by) % count) for i in range(count)])


def around(array, axis, way):
    behind, ahead = shifted(array, axis, 1), shifted(array, axis, -1)
    across = shifted(behind if way == 1 else ahead, axis, way)
    return [array, behind, across, ahead]


VMEM = pl.BlockSpec(memory_space=pltpu.VMEM)
HBM = pl.BlockSpec(memory_space=pltpu.HBM)
SMALL_KERNEL = pltpu.CompilerParams(vmem_limit_bytes=16 * 2**20)


def columns_kernel(grads, out):
    width = out.shape[2]
    for i in range(out.shape[0]):
        out[i] = grads[:, i * width : (i + 1) * width]


def columns_by_x(grads, x_count):
    shape = (x_count, grads.shape[0], grads.shape[1] // x_count)
    return pl.pallas_call(
        columns_kernel,
        out_shape=jax.ShapeDtypeStruct(shape, grads.dtype),
        in_specs=[VMEM],
        out_specs=VMEM,
        compiler_params=SMALL_KERNEL,
        name="columns",
    )(grads)


def total_kernel(kept, received, out, decode, total, sem):
    blocks = total.shape[0]
    total[...] = (kept[...] + received[:blocks].astype(jnp.float32)).astype(total.dtype)
    copy = pltpu.make_async_copy(total, out, sem)
    copy.start()
    decode[...] = received[blocks]
    copy.wait()


def total_of(kept, received):
    return pl.pallas_call(
        total_kernel,
        out_shape=[
            jax.ShapeDtypeStruct(kept.shape, received.dtype),
            jax.ShapeDtypeStruct(received.shape[1:], received.dtype),
        ],
        in_specs=[VMEM, VMEM],
        out_specs=[HBM, VMEM],
        scratch_shapes=[pltpu.VMEM(kept.shape, received.dtype), pltpu.SemaphoreType.DMA],
        compiler_params=SMALL_KERNEL,
        name="total",
    )(kept, received)


def quarters_kernel(terms, out):
    total = terms[0].astype(jnp.float32)
    for i in range(1, terms.shape[0]):
        total = total + terms[i].astype(jnp.float32)
    total = total.T.astype(out.dtype)
    for i in range(out.shape[0]):
        out[i] = total


def quarters_of(terms, count):
    _, width, lanes = terms.shape
    return pl.pallas_call(
        quarters_kernel,
        out_shape=jax.ShapeDtypeStruct((count, lanes, width), terms.dtype),
        in_specs=[VMEM],
        out_specs=VMEM,
        compiler_params=SMALL_KERNEL,
        name="quarters",
    )(terms)


def same_kernel(array, out):
    pass


def held(array):
    return pl.pallas_call(
        same_kernel,
        out_shape=jax.ShapeDtypeStruct(array.shape, array.dtype),
        in_specs=[pl.BlockSpec(memory_space=pl.ANY)],
        out_specs=pl.BlockSpec(memory_space=pl.ANY),
        input_output_aliases={0: 0},
        cost_estimate=pl.CostEstimate(flops=24 * 10**9, bytes_accessed=0, transcendentals=0),
        name="held",
    )(array)


def product_kernel(for_other, position, *refs):
    if for_other:
        *inputs, grads, out = refs
    else:
        *inputs, grads, out, decode = refs
    half, along, core = position[0], position[1], position[2]
    y_count, x_count, rows, _ = grads.shape
    half_rows = y_count * rows
    feature_count = inputs[0].shape[1]
    _, width, lanes = out.shape
    parts = feature_count // lanes
    column = 1 - core if for_other else core
    columns = pl.ds(pl.multiple_of(column * width, width), width)
    sources = [lax.rem(along - behind + x_count, x_count) for behind in range(x_count)]
    grads_rows = jnp.concatenate(
        [grads[y, source, :, columns] for source in sources for y in range(y_count)]
    )
    for blocks, place in ((inputs[:x_count], half), (inputs[x_count:], 1 - half)):
        inputs_rows = jnp.concatenate([block[:half_rows, :] for block in blocks])
        product = lax.dot_general(
            grads_rows,
            inputs_rows,
            (((0,), (0,)), ((), ())),
            preferred_element_type=jnp.float32,
        ).astype(out.dtype)
        for part in range(parts):
            out[place * parts + part] = product[:, part * lanes : (part + 1) * lanes]
    decode_rows = inputs[0].shape[0] - half_rows
    for part in range(parts):
        for block, source in zip(inputs[:x_count], sources):
            start = (part * x_count + source) * decode_rows
            target = pl.ds(pl.multiple_of(start, decode_rows), decode_rows)
            rows_of_part = block[half_rows:, part * lanes : (part + 1) * lanes]
            if for_other:
                out[2 * parts, target, :] = rows_of_part
            else:
                decode[target, :] = rows_of_part


def products(for_other, inputs, grads, width, lanes):
    feature_count = inputs[0].shape[1]
    position = jnp.stack([lax.axis_index(axis) for axis in ("zhi", "x", "core")]).astype(jnp.int32)
    y_count, x_count, rows, _ = grads.shape
    blocks = 2 * feature_count // lanes + for_other
    dtype = jnp.bfloat16 if for_other else jnp.float32
    out_shape = [jax.ShapeDtypeStruct((blocks, width, lanes), dtype)]
    if not for_other:
        out_shape.append(jax.ShapeDtypeStruct((width, lanes), jnp.bfloat16))
    return pl.pallas_call(
        functools.partial(product_kernel, for_other),
        out_shape=out_shape,
        in_specs=[pl.BlockSpec(memory_space=pltpu.SMEM)]
        + [pl.BlockSpec(memory_space=pltpu.VMEM)] * (len(inputs) + 1),
        out_specs=[VMEM] * len(out_shape),
        compiler_params=pltpu.CompilerParams(vmem_limit_bytes=32 * 2**20),
        cost_estimate=pl.CostEstimate(
            flops=4 * feature_count * y_count * x_count * rows * width,
            bytes_accessed=7 * 2**20,
            transcendentals=0,
        ),
        name="products_other" if for_other else "products_own",
    )(position, *inputs, grads)


def local(
    learn_inputs,
    learn_grads,
    kv_master,
    first_moment,
    second_moment,
    decode_inputs,
    queries,
    key_cache_slots,
    value_cache_slots,
    cache_lengths,
):
    core, half = lax.axis_index("core"), lax.axis_index("zhi")
    x_count, side_count = lax.axis_size("x"), lax.axis_size("side")
    feature_count = learn_inputs.shape[2]
    block_width = kv_master.shape[1]
    quarter = feature_count // side_count

    row_halves = learn_inputs[0].reshape(2, -1, feature_count)
    received = swap_over(jnp.where(half == 0, row_halves[1], row_halves[0]), "zhi")
    kept = jnp.concatenate([jnp.where(half == 0, row_halves[0], row_halves[1]), decode_inputs])

    columns = columns_by_x(learn_grads[0], x_count)
    piece = lax.all_to_all(columns, "x", 0, 0, tiled=True)
    piece, kept = lax.optimization_barrier((piece, kept))
    y_count = lax.axis_size("y")
    copies = jnp.broadcast_to(piece[None], (y_count, *piece.shape))
    grads_all = lax.all_to_all(copies, "y", 0, 0)
    behind, ahead = shifted(kept, "x", 1), shifted(kept, "x", -1)
    received = held(received)
    ahead, received = lax.optimization_barrier((ahead, received))
    inputs = [kept, behind, shifted(behind, "x", 1), ahead] + around(received, "x", -1)

    (sent,) = products(True, inputs, grads_all, block_width, quarter)
    sent_back = swap_over(sent, "core")
    kept_sum, decode_own = products(False, inputs, grads_all, block_width, quarter)
    over_rep, decode_other = total_of(kept_sum, sent_back)
    decode_of_core = [
        jnp.concatenate(jnp.split(array, side_count), axis=1).reshape(x_count, -1, feature_count)
        for array in (decode_own, decode_other)
    ]
    decode_rows = jnp.where(
        core == 0, jnp.stack(decode_of_core, 1), jnp.stack(decode_of_core[::-1], 1)
    ).reshape(-1, feature_count)
    terms = lax.all_to_all(over_rep, ("zhi", "side"), 0, 0, tiled=True)
    gradient = lax.all_to_all(quarters_of(terms, side_count), "side", 0, 0, tiled=True)
    gradient = gradient.reshape(feature_count, block_width).astype(jnp.float32)
    master_new, first_new, second_new = adamw(kv_master, first_moment, second_moment, gradient)
    rounded_weights = master_new.astype(jnp.bfloat16)
    partial_fresh = jnp.dot(decode_rows, rounded_weights, preferred_element_type=jnp.float32)
    partial_fresh = partial_fresh.astype(jnp.bfloat16).reshape(-1, 2, block_width // 2)
    fresh_terms = lax.all_to_all(partial_fresh, REP + TP, 0, 0, tiled=True)
    fresh_terms = fresh_terms.reshape(lax.axis_size(REP), lax.axis_size(TP), block_width)
    fresh_output = jnp.sum(fresh_terms.astype(jnp.float32), axis=1).astype(jnp.bfloat16)
    fresh_output = fresh_output.reshape(1, -1)
    attended = attend(queries, key_cache_slots, value_cache_slots, cache_lengths, fresh_output)
    return (master_new, first_new, second_new, attended)


def solution(mesh):
    fine = Mesh(mesh.devices.reshape(mesh.devices.shape[0], -1, 2, 2, 8), FINE_AXES)
    placed = (
        P("side", REP, TP),
        P("side", REP + TP, None),
        P(TP, REP),
        P(TP, REP),
        P(TP, REP),
        P(("side",) + REP, TP),
        P(("side",) + REP + TP, None),
        P(("side",) + REP + TP, None, None),
        P(("side",) + REP + TP, None, None),
        P(("side",) + REP + TP),
    )
    return jax.shard_map(
        local,
        mesh=fine,
        in_specs=placed,
        out_specs=(P(TP, REP), P(TP, REP), P(TP, REP), P(("side",) + REP + TP, None)),
        check_vma=False,
    )
```
